128 devices in a mesh: sample: 16 (over z_lo, y, core), head: 8 (over x, z_hi).
Axes of the slice: x: 4, y: 4, z: 4 (z_hi: 2, z_lo: 2; z = z_hi * 2 + z_lo), core: 2. Of those that a mesh axis runs over, the one named last changes fastest.
Arguments:
- queries: bfloat16 [16, 512, 8192], P('sample', None, 'head'), may hold values from -12 to 12
- suffix_keys: bfloat16 [16, 512, 1024], P('sample', None, 'head'), may hold values from -4 to 4
- suffix_values: bfloat16 [16, 512, 1024], P('sample', None, 'head'), may hold values from -16 to 16
- prefix_keys: bfloat16 [4096, 1024], P('sample', 'head'), may hold values from -6 to 6
- prefix_values: bfloat16 [4096, 1024], P('sample', 'head'), may hold values from -16 to 16
- lengths: int32 [16], replicated, may hold values from 1 to 512, as said below
- out_weight: bfloat16 [8192, 5120], P('head', 'sample'), may hold values from -0.0625 to 0.0625
Outputs:
- projected: bfloat16 [16, 512, 5120], P('sample', 'head')
The draws below stay inside these ranges and needn't reach their ends.
Inputs may be any that keep to these rules, and one draw needn't show every extreme that they name: `lengths`: some sample's length is exactly 512.
All inputs are finite; a program needn't handle non-finite values.
Results may differ from the reference program's by a relative error of at most 0.018.
Values may be sent and summed in bfloat16 or wider, within the bound.
No kernel may reach another device: no remote copies, remote signals or barrier semaphores. Data moves between devices by JAX's collectives and lax.ppermute only.
A program may use at most 128 MiB of HBM per device.

```python
import jax
import jax.numpy as jnp
from jax import lax

D = 5120
HQ = 64
KVH = 8
HD = 128
SUF = 512
SAMPLES = 16
PREFIX = 4096
N_HEAD = 8


def draw_prefix_keys(key, part):
    key = jax.random.fold_in(key, 1)
    return jnp.clip(jax.random.normal(key, (PREFIX, KVH * HD), jnp.float32), -4.0, 4.0).astype(jnp.bfloat16)


def draw_queries(key, part):
    key = jax.random.fold_in(key, 2)
    full_shape = (SAMPLES, SUF, HQ * HD)
    return jnp.clip(1.5 * jax.random.normal(key, full_shape, jnp.float32), -6.0, 6.0).astype(jnp.bfloat16)


def draw_lengths(key, part):
    key = jax.random.fold_in(key, 3)
    values = jax.random.randint(key, (SAMPLES,), 1, SUF + 1)
    longest = jax.random.randint(jax.random.fold_in(key, 7), (), 0, SAMPLES)
    return jnp.where(jnp.arange(SAMPLES) == longest, SUF, values).astype(jnp.int32)


def shard_levels(own_key, dims, cuts, least, high):
    factor_of, own = 1.0, jax.random.fold_in(own_key, 6)
    for position, shards_of in cuts:
        heights = jnp.exp(jax.random.uniform(jax.random.fold_in(own, position), (shards_of,), jnp.float32, least / len(cuts), high / len(cuts)))
        factor_of = factor_of * jnp.repeat(heights, dims[position] // shards_of).reshape([-1 if axis == position else 1 for axis in range(len(dims))])
    return factor_of


def centred(key, extent, scale, most, pieces=(), held_as=jnp.bfloat16):
    drawn = jax.random.normal(key, extent, jnp.float32) * scale
    if len(pieces) > 0:
        drawn = shard_levels(key, extent, pieces, -0.22, 0.18) * drawn
    return jnp.clip(drawn, min=-most, max=most).astype(held_as)


def setup_inputs(seed: int = 0) -> dict:
    streams_of = jax.random.split(jax.random.key(seed), 8)
    return {
        "queries": draw_queries(jax.random.fold_in(streams_of[7], 71), 0),
        "suffix_keys": centred(streams_of[1], (SAMPLES, SUF, KVH * HD), 1.0, 4.0, ((0, 16), (2, 8))),
        "suffix_values": jnp.clip(jax.random.uniform(streams_of[2], (SAMPLES, SUF, KVH * HD), jnp.float32, -16.0, 16.0) * shard_levels(streams_of[2], (SAMPLES, SUF, KVH * HD), ((0, 16), (2, 8)), -0.4, 0.0), -16.0, 16.0).astype(jnp.bfloat16),
        "prefix_keys": draw_prefix_keys(jax.random.fold_in(streams_of[7], 71), 0),
        "prefix_values": jnp.clip(jax.random.uniform(streams_of[4], (PREFIX, KVH * HD), jnp.float32, -16.0, 16.0) * shard_levels(streams_of[4], (PREFIX, KVH * HD), ((0, 16), (1, 8)), -0.4, 0.0), -16.0, 16.0).astype(jnp.bfloat16),
        "lengths": draw_lengths(jax.random.fold_in(streams_of[7], 71), 0),
        "out_weight": centred(streams_of[6], (HQ * HD, D), (HQ * HD) ** -0.5, 0.0625, ((0, 8), (1, 16))),
    }


def sample_attention(query_rows, key_rows, value_rows, length):
    group_size = HQ // KVH
    grouped = query_rows.astype(jnp.float32).reshape(SUF, KVH, group_size, HD)
    keyed_rows = key_rows.astype(jnp.float32).reshape(PREFIX + SUF, KVH, HD)
    valued_rows = value_rows.astype(jnp.float32).reshape(PREFIX + SUF, KVH, HD)
    row_ids = jnp.arange(SUF, dtype=jnp.int32)[:, None]
    key_ids = jnp.arange(PREFIX + SUF, dtype=jnp.int32)[None, :] - PREFIX
    visible = key_ids <= row_ids

    def one_head(head_index):
        query_head = lax.dynamic_index_in_dim(grouped, head_index, 1, keepdims=False)
        key_head = lax.dynamic_index_in_dim(keyed_rows, head_index, 1, keepdims=False)
        value_head = lax.dynamic_index_in_dim(valued_rows, head_index, 1, keepdims=False)
        scores = jnp.einsum("qgd,kd->gqk", query_head, key_head, precision=lax.Precision.HIGHEST) * (HD ** -0.5)
        scores = jnp.where(visible[None], scores, -jnp.inf)
        row_max = jnp.max(scores, axis=-1, keepdims=True)
        weights = jnp.exp(scores - row_max)
        row_sum = jnp.sum(weights, axis=-1, keepdims=True)
        rounded = lax.optimization_barrier(weights.astype(jnp.bfloat16)).astype(jnp.float32)
        summed = jnp.einsum("gqk,kd->gqd", rounded, value_head, precision=lax.Precision.HIGHEST)
        return summed / row_sum

    head_outputs = lax.map(one_head, jnp.arange(KVH, dtype=jnp.int32))
    arranged = jnp.transpose(head_outputs, (2, 0, 1, 3)).reshape(SUF, HQ * HD)
    live_rows = (jnp.arange(SUF, dtype=jnp.int32) < length)[:, None]
    return jnp.where(live_rows, arranged, 0.0).astype(jnp.bfloat16)


def reference(queries, suffix_keys, suffix_values, prefix_keys, prefix_values, lengths, out_weight):
    group_width = HQ * HD // N_HEAD

    def one_sample(sample_index):
        own_queries = lax.dynamic_index_in_dim(queries, sample_index, 0, keepdims=False)
        key_rows = jnp.concatenate([prefix_keys, lax.dynamic_index_in_dim(suffix_keys, sample_index, 0, keepdims=False)], axis=0)
        value_rows = jnp.concatenate([prefix_values, lax.dynamic_index_in_dim(suffix_values, sample_index, 0, keepdims=False)], axis=0)
        length = lax.dynamic_index_in_dim(lengths, sample_index, 0, keepdims=False)
        attended = sample_attention(own_queries, key_rows, value_rows, length)
        running = jnp.zeros((SUF, D), jnp.float32)
        for group_index in range(N_HEAD):
            group_part = jnp.dot(attended[:, group_index * group_width:(group_index + 1) * group_width], out_weight[group_index * group_width:(group_index + 1) * group_width], preferred_element_type=jnp.float32)
            running = running + lax.optimization_barrier(group_part.astype(jnp.bfloat16)).astype(jnp.float32)
        return running.astype(jnp.bfloat16)

    return lax.map(one_sample, jnp.arange(SAMPLES, dtype=jnp.int32))
```

```python
import functools
import math

import jax
import jax.numpy as jnp
from jax import lax
from jax.experimental import pallas as pl
from jax.experimental.pallas import tpu as pltpu
from jax.sharding import PartitionSpec as P

HD = 128
HEADS = 4
TILE = 256
SCALE = HD ** (-0.5) * math.log2(math.e)
BF = jnp.bfloat16
F32 = jnp.float32
NT = (((1,), (1,)), ((), ()))


def sample_pairs(to):
    place = lambda z, y, c: (z * 4 + y) * 2 + c
    return [
        (place(z, y, c), place(*to(z, y, c)))
        for z in range(2) for y in range(4) for c in range(2)
    ]


def head_pairs(to):
    pairs = []
    for x in range(4):
        for z in range(2):
            tx, tz = to(x, z)
            pairs.append((x * 2 + z, tx * 2 + tz))
    return pairs


CORE = sample_pairs(lambda z, y, c: (z, y, 1 - c))
ZLO = sample_pairs(lambda z, y, c: (1 - z, y, c))
YUP = sample_pairs(lambda z, y, c: (z, (y + 1) % 4, c))
YDOWN = sample_pairs(lambda z, y, c: (z, (y + 3) % 4, c))
YFAR = sample_pairs(lambda z, y, c: (z, (y + 2) % 4, c))
XUP = head_pairs(lambda x, z: ((x + 1) % 4, z))
XDOWN = head_pairs(lambda x, z: ((x + 3) % 4, z))
ZHI = head_pairs(lambda x, z: (x, 1 - z))


def over_sample(value, pairs):
    return lax.ppermute(value, "sample", pairs)


def over_head(value, pairs):
    return lax.ppermute(value, "head", pairs)


def attend_kernel(counts, first, last, lens_ref, q_ref, *refs):
    refs = list(refs)
    suffix_ref = refs.pop(0) if first else None
    kv_refs = [refs.pop(0) for _ in counts]
    acc_in, stat_in = (None, None) if first else (refs.pop(0), refs.pop(0))
    if last:
        out_ref = refs.pop(0)
    else:
        acc_out, stat_out = refs.pop(0), refs.pop(0)
    keys_ref, values_ref = refs.pop(0), refs.pop(0)
    sample, tile = pl.program_id(0), pl.program_id(1)
    rows_total = keys_ref.shape[0]

    @pl.when((sample == 0) & (tile == 0))
    def _():
        at = 0
        for kv_ref, count in zip(kv_refs, counts):
            for b in range(count):
                block = kv_ref[b]
                rows = block.shape[0]
                keys_ref[at:at + rows] = block[:, :HD]
                values_ref[at:at + rows, :HD] = block[:, HD:]
                at += rows
        values_ref[:, HD:] = jnp.ones((rows_total, HD), BF)

    length = lens_ref[sample]
    live = tile * TILE < length

    def fold(state, scores, values):
        top = jnp.max(scores, axis=1, keepdims=True)
        if state is None:
            weights = jnp.exp2(scores - top)
            return top, jnp.dot(weights.astype(BF), values, preferred_element_type=F32)
        old, acc = state
        top = jnp.maximum(old, top)
        weights = jnp.exp2(scores - top)
        part = jnp.dot(weights.astype(BF), values, preferred_element_type=F32)
        return top, acc * jnp.exp2(old - top) + part

    def body(tile_static):
        for h in range(HEADS):
            cols = slice(h * HD, (h + 1) * HD)
            q = (q_ref[:, cols].astype(F32) * SCALE).astype(BF)
            if first:
                row = lax.broadcasted_iota(jnp.int32, (TILE, TILE), 0)
                col = lax.broadcasted_iota(jnp.int32, (TILE, TILE), 1)
                state = None
                for t in range(tile_static, -1, -1):
                    block = suffix_ref[t * TILE:(t + 1) * TILE]
                    scores = lax.dot_general(q, block[:, :HD], NT, preferred_element_type=F32)
                    if t == tile_static:
                        scores = jnp.where(col <= row, scores, -1e30)
                    values = jnp.concatenate([block[:, HD:], jnp.ones((TILE, HD), BF)], 1)
                    state = fold(state, scores, values)
            else:
                state = None
            at = 0
            while at < rows_total:
                size = TILE if first else rows_total
                scores = lax.dot_general(q, keys_ref[at:at + size], NT, preferred_element_type=F32)
                state = fold(state, scores, values_ref[at:at + size])
                at += size
            top, acc = state
            num, den = acc[:, :HD], acc[:, HD:]
            if not first:
                top = jnp.broadcast_to(top, (TILE, HD))
                old = jnp.broadcast_to(stat_in[:, h:h + 1], (TILE, HD))
                total = jnp.broadcast_to(stat_in[:, HEADS + h:HEADS + h + 1], (TILE, HD))
                new = jnp.maximum(old, top)
                keep, add = jnp.exp2(old - new), jnp.exp2(top - new)
                num = acc_in[:, cols] * keep + num * add
                den = total * keep + den * add
                top = new[:, :1]
            if last:
                row = tile * TILE + lax.broadcasted_iota(jnp.int32, (TILE, HD), 0)
                out_ref[:, cols] = jnp.where(row < length, num / den, 0.0).astype(BF)
            else:
                acc_out[:, cols] = num
                stat_out[:, h:h + 1] = top
                stat_out[:, HEADS + h:HEADS + h + 1] = den[:, :1]

    if first:
        for t in range(2):
            pl.when(live & (tile == t))(functools.partial(body, t))
    else:
        pl.when(live)(functools.partial(body, 0))

    if last:
        @pl.when(jnp.logical_not(live))
        def _():
            out_ref[...] = jnp.zeros_like(out_ref)


def attend(lens, q, suffix, kvs, state, last):
    first = state is None
    samples, rows, width = q.shape
    counts = [kv.shape[0] for kv in kvs]
    keys_total = sum(kv.shape[0] * kv.shape[1] for kv in kvs)
    tiled = lambda w: pl.BlockSpec((None, TILE, w), lambda s, t, _: (s, t, 0))
    in_specs = [tiled(width)]
    args = [q]
    if first:
        in_specs.append(pl.BlockSpec((None, rows, 2 * HD), lambda s, t, _: (s, 0, 0)))
        args.append(suffix)
    for kv in kvs:
        in_specs.append(pl.BlockSpec(kv.shape, lambda s, t, _: (0, 0, 0)))
        args.append(kv)
    if not first:
        in_specs += [tiled(width), tiled(HD)]
        args += list(state)
    if last:
        out_specs = tiled(width)
        out_shape = jax.ShapeDtypeStruct((samples, rows, width), BF)
    else:
        out_specs = [tiled(width), tiled(HD)]
        out_shape = [
            jax.ShapeDtypeStruct((samples, rows, width), F32),
            jax.ShapeDtypeStruct((samples, rows, HD), F32),
        ]
    keys_seen = keys_total + (rows // 2 if first else 0)
    return pl.pallas_call(
        functools.partial(attend_kernel, counts, first, last),
        grid_spec=pltpu.PrefetchScalarGridSpec(
            num_scalar_prefetch=1,
            grid=(samples, rows // TILE),
            in_specs=in_specs,
            out_specs=out_specs,
            scratch_shapes=[
                pltpu.VMEM((keys_total, HD), BF),
                pltpu.VMEM((keys_total, 2 * HD), BF),
            ],
        ),
        out_shape=out_shape,
        name="attend_first" if first else "attend_last" if last else "attend_more",
        cost_estimate=pl.CostEstimate(
            flops=samples * rows * HEADS * keys_seen * HD * 8,
            bytes_accessed=8 * 2**20,
            transcendentals=samples * rows * HEADS * keys_seen,
        ),
        compiler_params=pltpu.CompilerParams(vmem_limit_bytes=48 * 2**20),
    )(lens, *args)


def project_kernel(count, spans, place_ref, w_own_ref, w_other_ref, *refs):
    own_refs, other_refs = refs[:count], refs[count:2 * count]
    add_refs, out_ref = refs[2 * count:-1], refs[-1]
    tile = pl.program_id(0)
    own = jnp.concatenate([ref[s] for ref in own_refs for s in (0, 1)], axis=0)
    other = jnp.concatenate([ref[s] for ref in other_refs for s in (1, 0)], axis=0)
    acc = lax.dot_general(w_own_ref[...], own, NT, preferred_element_type=F32)
    acc = acc + lax.dot_general(w_other_ref[...], other, NT, preferred_element_type=F32)
    partial = []
    for ref, (_, start, tiles, whole) in zip(add_refs, spans):
        if whole:
            acc = acc + ref[...].astype(F32)
        else:
            partial.append((ref, start, tiles))
    out_ref[...] = acc.astype(BF)
    for ref, start, tiles in partial:
        @pl.when((tile >= start) & (tile < start + tiles))
        def _():
            out_ref[...] = (acc + ref[...].astype(F32)).astype(BF)


def project(place, weight, rows_own, rows_other, first, tiles, size, blocks, adds, name):
    depth = rows_own.shape[3]
    lanes = 2 * rows_own.shape[2] * len(blocks)

    def rows_spec(step, own):
        def index(i, p):
            z = p[1] if own else 1 - p[1]
            return (0, 2 * lax.rem(p[0] + step, 4) + z, 0, 0)

        return pl.BlockSpec((2, None, rows_own.shape[2], depth), index)

    def add_spec(lane, start, count):
        return pl.BlockSpec(
            (size, lanes), lambda i, p: (jnp.clip(i - start, 0, count - 1), lane)
        )

    spans = [(lane, start, count, count == tiles) for _, lane, start, count in adds]
    in_specs = [
        pl.BlockSpec((size, depth), lambda i, p: (first + i, p[2])),
        pl.BlockSpec((size, depth), lambda i, p: (first + i, 1 - p[2])),
    ]
    in_specs += [rows_spec(*block) for block in blocks] * 2
    in_specs += [add_spec(lane, start, count) for _, lane, start, count in adds]
    return pl.pallas_call(
        functools.partial(project_kernel, len(blocks), spans),
        grid_spec=pltpu.PrefetchScalarGridSpec(
            num_scalar_prefetch=1,
            grid=(tiles,),
            in_specs=in_specs,
            out_specs=pl.BlockSpec((size, lanes), lambda i, p: (i, 0)),
        ),
        out_shape=jax.ShapeDtypeStruct((tiles * size, lanes), BF),
        name=name,
        cost_estimate=pl.CostEstimate(
            flops=4 * tiles * size * lanes * depth,
            bytes_accessed=4 * tiles * size * depth + 2 * tiles * size * lanes,
            transcendentals=0,
        ),
        compiler_params=pltpu.CompilerParams(vmem_limit_bytes=32 * 2**20),
    )(place, weight, weight, *([rows_own] * len(blocks)), *([rows_other] * len(blocks)), *[a[0] for a in adds])


def finish_kernel(cols, place_ref, own_ref, got_ref, out_ref):
    own = own_ref[...].astype(F32)[:, :64]
    got = got_ref[...].astype(F32)[:, 64:]
    first = place_ref[2] == 0
    even = jnp.where(first, own, got)
    odd = jnp.where(first, got, own)
    both = jnp.concatenate([even, odd], axis=0)
    out_ref[...] = jnp.transpose(both).astype(BF)


def finish(place, own, got, cols):
    blocks = own.shape[0] // cols
    part = pl.BlockSpec((cols, 128), lambda i, p: (i, 0))
    return pl.pallas_call(
        functools.partial(finish_kernel, cols),
        grid_spec=pltpu.PrefetchScalarGridSpec(
            num_scalar_prefetch=1,
            grid=(blocks,),
            in_specs=[part, part],
            out_specs=pl.BlockSpec((64, 2 * cols), lambda i, p: (0, i)),
        ),
        out_shape=jax.ShapeDtypeStruct((64, 2 * cols * blocks), BF),
        name="finish",
    )(place, own, got)


PARITY = [[i for i in range(16) if i % 2 == c] for c in range(2)]
SIZE = 256
EARLY, LATE = 6, 4


def per_device(
    queries, suffix_keys, suffix_values, prefix_keys, prefix_values, lengths, out_weight
):
    sample = lax.axis_index("sample")
    head = lax.axis_index("head")
    core = sample % 2
    x, z_hi = head // 2, head % 2
    place = jnp.stack([x, z_hi, core]).astype(jnp.int32)

    weight = lax.all_gather(out_weight.T, "sample", axis=0, tiled=True, axis_index_groups=PARITY)

    lens = jnp.stack([lengths[sample], lengths[sample + 1 - 2 * core]])
    kv = jnp.concatenate([prefix_keys, prefix_values], axis=1)
    suffix = jnp.concatenate([suffix_keys[0], suffix_values[0]], axis=1)
    width = queries.shape[2] // 2
    mine = lax.dynamic_slice_in_dim(queries[0], core * width, width, axis=1)
    theirs = lax.dynamic_slice_in_dim(queries[0], (1 - core) * width, width, axis=1)

    kv_z = over_sample(kv, ZLO)
    kv_core = over_sample(kv, CORE)
    q = jnp.stack([mine, over_sample(theirs, CORE)])
    suffixes = jnp.stack([suffix, over_sample(suffix, CORE)])
    near = jnp.stack([kv, kv_z])
    ys = [over_sample(near, to) for to in (YUP, YDOWN, YFAR)]

    state = attend(lens, q, suffixes, [jnp.stack([kv, kv_core])], None, False)
    ys, state = lax.optimization_barrier((ys, state))
    rest = [kv_z[None]] + ys
    rest_core = [over_sample(block, CORE) for block in rest]
    state = attend(lens, q, None, rest, state, False)
    half = attend(lens, q, None, rest_core, state, True)

    half_core = over_sample(half, CORE)
    half = half.reshape(2, 8, 64, width)
    half_core = half_core.reshape(2, 8, 64, width)

    def early(blocks, adds, name):
        return project(place, weight, half, half_core, 0, EARLY, SIZE, blocks, adds, name)

    def late(blocks, adds, name):
        return project(place, weight, half, half_core, EARLY, LATE, SIZE, blocks, adds, name)

    def halves(array):
        lines = array.shape[0] // 2
        return over_head(array[:lines], XUP), over_head(array[lines:], XDOWN)

    OTHER, OWN = False, True
    both_z = lambda step: [(step, OTHER), (step, OWN)]
    he, hl = EARLY // 2, LATE // 2

    got = over_head(late([(s, OTHER) for s in range(4)], [], "late_give"), ZHI)
    via_up, via_down = halves(early(both_z(2), [], "early_far"))
    below = over_head(early(both_z(1), [(via_up, 0, 0, he)], "early_up"), XUP)
    above = over_head(early(both_z(3), [(via_down, 0, he, he)], "early_down"), XDOWN)
    lvia_up, lvia_down = halves(late([(2, OWN)], [(got, 2, 0, LATE)], "late_far"))
    whole = (0, EARLY)
    give = early([(0, OTHER)], [(below, 0, *whole), (above, 0, *whole)], "early_give")
    from_z = over_head(give, ZHI)
    lbelow = over_head(
        late([(1, OWN)], [(got, 1, 0, LATE), (lvia_up, 0, 0, hl)], "late_up"), XUP
    )
    labove = over_head(
        late([(3, OWN)], [(got, 3, 0, LATE), (lvia_down, 0, hl, hl)], "late_down"), XDOWN
    )
    early_sum = early(
        [(0, OWN)], [(below, 1, *whole), (above, 1, *whole), (from_z, 0, *whole)], "early_sum"
    )
    late_sum = late(
        [(0, OWN)], [(got, 0, 0, LATE), (lbelow, 0, 0, LATE), (labove, 0, 0, LATE)], "late_sum"
    )

    done = jnp.concatenate([early_sum, late_sum], axis=0)
    return finish(place, done, over_sample(done, CORE), out_weight.shape[1])[None]


def solution(mesh):
    placed = (
        P("sample", None, "head"),
        P("sample", None, "head"),
        P("sample", None, "head"),
        P("sample", "head"),
        P("sample", "head"),
        P(),
        P("head", "sample"),
    )
    return jax.shard_map(
        per_device, mesh=mesh, in_specs=placed, out_specs=P("sample", "head", None), check_vma=False
    )
```

```python
import functools
import math

import jax
import jax.numpy as jnp
from jax import lax
from jax.experimental import pallas as pl
from jax.experimental.pallas import tpu as pltpu
from jax.sharding import PartitionSpec as P

HD = 128
HEADS = 4
TILE = 256
SCALE = HD ** (-0.5) * math.log2(math.e)
BF = jnp.bfloat16
F32 = jnp.float32
NT = (((1,), (1,)), ((), ()))


def sample_pairs(to):
    place = lambda z, y, c: (z * 4 + y) * 2 + c
    return [
        (place(z, y, c), place(*to(z, y, c)))
        for z in range(2) for y in range(4) for c in range(2)
    ]


def head_pairs(to):
    pairs = []
    for x in range(4):
        for z in range(2):
            tx, tz = to(x, z)
            pairs.append((x * 2 + z, tx * 2 + tz))
    return pairs


CORE = sample_pairs(lambda z, y, c: (z, y, 1 - c))
ZLO = sample_pairs(lambda z, y, c: (1 - z, y, c))
YUP = sample_pairs(lambda z, y, c: (z, (y + 1) % 4, c))
YDOWN = sample_pairs(lambda z, y, c: (z, (y + 3) % 4, c))
YFAR = sample_pairs(lambda z, y, c: (z, (y + 2) % 4, c))
XUP = head_pairs(lambda x, z: ((x + 1) % 4, z))
XDOWN = head_pairs(lambda x, z: ((x + 3) % 4, z))
ZHI = head_pairs(lambda x, z: (x, 1 - z))


def over_sample(value, pairs):
    return lax.ppermute(value, "sample", pairs)


def over_head(value, pairs):
    return lax.ppermute(value, "head", pairs)


X, Z_HI, CORE_AT, Y, Z_LO, LENGTH = range(6)


def attend_kernel(counts, samples, first, last, place_ref, q_own_ref, q_got_ref, *refs):
    refs = list(refs)
    suffix_refs = [refs.pop(0) for _ in range(4)] if first else None
    kv_refs = [refs.pop(0) for _ in counts]
    acc_in, stat_in = (None, None) if first else (refs.pop(0), refs.pop(0))
    if last:
        out_ref = refs.pop(0)
    else:
        acc_out, stat_out = refs.pop(0), refs.pop(0)
    keys_ref, values_ref = refs.pop(0), refs.pop(0)
    step, tile = pl.program_id(0), pl.program_id(1)
    sample = samples[0] + step
    rows_total = keys_ref.shape[0]

    @pl.when((step == 0) & (tile == 0))
    def _():
        at = 0
        for kv_ref, count in zip(kv_refs, counts):
            for b in range(count):
                block = kv_ref[b]
                rows = block.shape[0]
                keys_ref[at:at + rows] = block[:, :HD]
                values_ref[at:at + rows, :HD] = block[:, HD:]
                at += rows
        values_ref[:, HD:] = jnp.ones((rows_total, HD), BF)

    length = place_ref[LENGTH + sample]
    live = tile * TILE < length

    def pick(own, got):
        if len(samples) == 1:
            return got if samples[0] else own
        return jnp.where(sample == 0, own, got)

    def fold(state, scores, values):
        top = jnp.max(scores, axis=1, keepdims=True)
        if state is None:
            weights = jnp.exp2(scores - top)
            return top, jnp.dot(weights.astype(BF), values, preferred_element_type=F32)
        old, acc = state
        top = jnp.maximum(old, top)
        weights = jnp.exp2(scores - top)
        part = jnp.dot(weights.astype(BF), values, preferred_element_type=F32)
        return top, acc * jnp.exp2(old - top) + part

    def body(tile_static):
        for h in range(HEADS):
            cols = slice(h * HD, (h + 1) * HD)
            q = pick(q_own_ref[:, cols].astype(F32), q_got_ref[:, cols].astype(F32))
            q = (q * SCALE).astype(BF)
            state = None
            if first:
                row = lax.broadcasted_iota(jnp.int32, (TILE, TILE), 0)
                col = lax.broadcasted_iota(jnp.int32, (TILE, TILE), 1)
                for t in range(tile_static, -1, -1):
                    lines = slice(t * TILE, (t + 1) * TILE)
                    keys, values = (
                        pick(suffix_refs[i][lines], suffix_refs[i + 2][lines]) for i in (0, 1)
                    )
                    scores = lax.dot_general(q, keys, NT, preferred_element_type=F32)
                    if t == tile_static:
                        scores = jnp.where(col <= row, scores, -1e30)
                    values = jnp.concatenate([values, jnp.ones((TILE, HD), BF)], 1)
                    state = fold(state, scores, values)
            at = 0
            size = TILE if first else rows_total
            while at < rows_total:
                scores = lax.dot_general(q, keys_ref[at:at + size], NT, preferred_element_type=F32)
                state = fold(state, scores, values_ref[at:at + size])
                at += size
            top, acc = state
            num, den = acc[:, :HD], acc[:, HD:]
            if not first:
                top = jnp.broadcast_to(top, (TILE, HD))
                old = jnp.broadcast_to(stat_in[:, h:h + 1], (TILE, HD))
                total = jnp.broadcast_to(stat_in[:, HEADS + h:HEADS + h + 1], (TILE, HD))
                new = jnp.maximum(old, top)
                keep, add = jnp.exp2(old - new), jnp.exp2(top - new)
                num = acc_in[:, cols] * keep + num * add
                den = total * keep + den * add
                top = new[:, :1]
            if last:
                row = tile * TILE + lax.broadcasted_iota(jnp.int32, (TILE, HD), 0)
                out_ref[:, cols] = jnp.where(row < length, num / den, 0.0).astype(BF)
            else:
                acc_out[:, cols] = num
                stat_out[:, h:h + 1] = top
                stat_out[:, HEADS + h:HEADS + h + 1] = den[:, :1]

    if first:
        for t in range(2):
            pl.when(live & (tile == t))(functools.partial(body, t))
    else:
        pl.when(live)(functools.partial(body, 0))

    if last:
        @pl.when(jnp.logical_not(live))
        def _():
            out_ref[...] = jnp.zeros_like(out_ref)


def attend(place, q_own, q_got, suffixes, kvs, state, samples, last, name):
    first = state is None
    rows, width = q_got.shape[0], q_got.shape[1] // 2
    counts = [kv.shape[0] for kv in kvs]
    keys_total = sum(kv.shape[0] * kv.shape[1] for kv in kvs)
    tiled = lambda w, base: pl.BlockSpec((None, TILE, w), lambda s, t, p: (base + s, t, 0))
    whole = lambda a: pl.BlockSpec(a.shape, lambda s, t, p: (0,) * a.ndim)
    in_specs = [
        pl.BlockSpec((TILE, width), lambda s, t, p: (t, p[CORE_AT])),
        pl.BlockSpec((TILE, width), lambda s, t, p: (t, p[CORE_AT])),
    ]
    args = [q_own, q_got]
    for array in ([*suffixes] if first else []) + kvs:
        in_specs.append(whole(array))
        args.append(array)
    if not first:
        in_specs += [tiled(width, samples[0]), tiled(HD, samples[0])]
        args += list(state)
    count = len(samples)
    if last:
        out_specs = tiled(width, 0)
        out_shape = jax.ShapeDtypeStruct((count, rows, width), BF)
    else:
        out_specs = [tiled(width, 0), tiled(HD, 0)]
        out_shape = [
            jax.ShapeDtypeStruct((count, rows, width), F32),
            jax.ShapeDtypeStruct((count, rows, HD), F32),
        ]
    keys_seen = keys_total + (rows // 2 if first else 0)
    return pl.pallas_call(
        functools.partial(attend_kernel, counts, samples, first, last),
        grid_spec=pltpu.PrefetchScalarGridSpec(
            num_scalar_prefetch=1,
            grid=(count, rows // TILE),
            in_specs=in_specs,
            out_specs=out_specs,
            scratch_shapes=[
                pltpu.VMEM((keys_total, HD), BF),
                pltpu.VMEM((keys_total, 2 * HD), BF),
            ],
        ),
        out_shape=out_shape,
        name=name,
        cost_estimate=pl.CostEstimate(
            flops=count * rows * HEADS * keys_seen * HD * 32,
            bytes_accessed=4 * count * 2**20,
            transcendentals=count * rows * HEADS * keys_seen,
        ),
        compiler_params=pltpu.CompilerParams(vmem_limit_bytes=48 * 2**20),
    )(place, *args)


OTHER, OWN = False, True


def project_kernel(tiles, count, spans, place_ref, *refs):
    weight_refs = refs[:2 * tiles]
    rows_refs = refs[2 * tiles:2 * tiles + 4 * count]
    add_refs, out_ref = refs[2 * tiles + 4 * count:-1], refs[-1]
    tile = pl.program_id(0)
    own = jnp.concatenate([r[...] for b in range(count) for r in rows_refs[4 * b:4 * b + 2]], axis=0)
    other = jnp.concatenate(
        [r[...] for b in range(count) for r in rows_refs[4 * b + 2:4 * b + 4]], axis=0
    )

    def body(at):
        acc = lax.dot_general(weight_refs[2 * at][...], own, NT, preferred_element_type=F32)
        acc += lax.dot_general(weight_refs[2 * at + 1][...], other, NT, preferred_element_type=F32)
        for ref, (start, length) in zip(add_refs, spans):
            if start <= at < start + length:
                acc += ref[...].astype(F32)
        out_ref[...] = acc.astype(BF)

    for at in range(tiles):
        pl.when(tile == at)(functools.partial(body, at))


def project(place, weights, rows, blocks, adds, name):
    tiles = len(weights)
    size = weights[0].shape[0]
    part, depth = rows[0].shape[1:]
    lanes = 2 * part * len(blocks)

    def rows_spec(step, own):
        def index(i, p):
            z = p[Z_HI] if own else 1 - p[Z_HI]
            return (2 * lax.rem(p[X] + step, 4) + z, 0, 0)

        return pl.BlockSpec((None, part, depth), index)

    def add_spec(lane, start, count):
        return pl.BlockSpec(
            (size, lanes), lambda i, p: (jnp.clip(i - start, 0, count - 1), lane)
        )

    in_specs, args = [], []
    for weight in weights:
        in_specs.append(pl.BlockSpec((size, depth), lambda i, p: (0, p[CORE_AT])))
        in_specs.append(pl.BlockSpec((size, depth), lambda i, p: (0, 1 - p[CORE_AT])))
        args += [weight, weight]
    for block in blocks:
        in_specs += [rows_spec(*block)] * 4
        args += rows
    for array, lane, start, count in adds:
        in_specs.append(add_spec(lane, start, count))
        args.append(array)
    return pl.pallas_call(
        functools.partial(project_kernel, tiles, len(blocks), [a[2:] for a in adds]),
        grid_spec=pltpu.PrefetchScalarGridSpec(
            num_scalar_prefetch=1,
            grid=(tiles,),
            in_specs=in_specs,
            out_specs=pl.BlockSpec((size, lanes), lambda i, p: (i, 0)),
        ),
        out_shape=jax.ShapeDtypeStruct((tiles * size, lanes), BF),
        name=name,
        cost_estimate=pl.CostEstimate(
            flops=4 * tiles * size * lanes * depth,
            bytes_accessed=4 * tiles * size * depth + 2 * tiles * size * lanes,
            transcendentals=0,
        ),
        compiler_params=pltpu.CompilerParams(vmem_limit_bytes=32 * 2**20),
    )(place, *args)


def sum_over_head(place, weights, rows, tag):
    run = lambda w, blocks, adds, name: project(place, w, rows, blocks, adds, name + tag)
    both = lambda step: [(step, OTHER), (step, OWN)]
    n = len(weights) // 2
    top, low = weights[:n], weights[n:]
    via_up = over_head(run(top, both(2), [], "far_top"), XUP)
    via_down = over_head(run(low, both(2), [], "far_low"), XDOWN)
    below_low = over_head(run(low, both(1), [], "up_low"), XUP)
    above_top = over_head(run(top, both(3), [], "down_top"), XDOWN)
    below_top = over_head(run(top, both(1), [(via_up, 0, 0, n)], "up_top"), XUP)
    last = run(low, both(3), [(via_down, 0, 0, n)], "down_low")
    above_low = over_head(last, XDOWN)

    def arrived(lane):
        return [
            (below_top, lane, 0, n), (above_top, lane, 0, n),
            (below_low, lane, n, n), (above_low, lane, n, n),
        ]

    from_z = over_head(run(weights, [(0, OTHER)], arrived(0), "give"), ZHI)
    return run(weights, [(0, OWN)], arrived(1) + [(from_z, 0, 0, 2 * n)], "sum"), last


SPOTS = ((0, 3, 4, 2), (1, 7, 5, 6))


def finish_kernel(cols, blocks, place_ref, spot_ref, *refs):
    own_refs, got_refs, out_ref = refs[:2], refs[2:4], refs[4]
    lane = lax.broadcasted_iota(jnp.int32, (64, 128), 1)
    row = lax.broadcasted_iota(jnp.int32, (64, 128), 0)
    turn = lambda array, at: lax.dot_general(
        jnp.where(lane == row + at, 1.0, 0.0).astype(BF), array, NT, preferred_element_type=F32
    )
    first = place_ref[CORE_AT] == 0
    count = len(SPOTS) * len(SPOTS[0]) // 2
    for b in range(blocks):
        i = pl.program_id(0) * blocks + b
        dz = lax.rem(i // 4 + place_ref[Z_LO], 2)
        dy = lax.rem(lax.rem(i, 4) + 4 - place_ref[Y], 4)
        spot = spot_ref[dz * 4 + dy]
        lines = pl.ds(pl.multiple_of(lax.rem(spot, count) * cols, cols), cols)
        take = lambda pair: jnp.where(spot < count, pair[0][lines], pair[1][lines])
        own, got = turn(take(own_refs), 0), turn(take(got_refs), 64)
        even, odd = jnp.where(first, own, got), jnp.where(first, got, own)
        out_ref[:, b * 2 * cols:(b + 1) * 2 * cols] = jnp.concatenate([even, odd], axis=1).astype(BF)


def finish(place, own, got, cols):
    spots = jnp.array([s for line in SPOTS for s in line], jnp.int32)
    whole = pl.BlockSpec(own[0].shape, lambda i, p, s: (0, 0))
    blocks = 4
    return pl.pallas_call(
        functools.partial(finish_kernel, cols, blocks),
        grid_spec=pltpu.PrefetchScalarGridSpec(
            num_scalar_prefetch=2,
            grid=(8 // blocks,),
            in_specs=[whole] * 4,
            out_specs=pl.BlockSpec((64, blocks * 2 * cols), lambda i, p, s: (0, i)),
        ),
        out_shape=jax.ShapeDtypeStruct((64, 16 * cols), BF),
        name="finish",
    )(place, spots, *own, *got)


def per_device(
    queries, suffix_keys, suffix_values, prefix_keys, prefix_values, lengths, out_weight
):
    hold = lax.optimization_barrier
    sample = lax.axis_index("sample")
    head = lax.axis_index("head")
    core = sample % 2
    width = queries.shape[2] // 2
    place = jnp.stack([
        head // 2, head % 2, core, (sample // 2) % 4, sample // 8,
        lengths[sample], lengths[sample + 1 - 2 * core],
    ]).astype(jnp.int32)

    kv = jnp.concatenate([prefix_keys, prefix_values], axis=1)
    kv_z = over_sample(kv, ZLO)
    q_own = queries[0]
    q_got = over_sample(q_own, CORE)
    suffix = [suffix_keys[0], suffix_values[0]]
    suffixes = suffix + [over_sample(a, CORE) for a in suffix]
    kv_core = over_sample(kv, CORE)
    near = jnp.stack([kv, kv_z])
    ys = [over_sample(near, to) for to in (YUP, YDOWN, YFAR)]

    w, near = hold((out_weight.T, near))
    w_z = over_sample(w, ZLO)

    run = lambda kvs, state, samples, last, name: attend(
        place, q_own, q_got, suffixes, kvs, state, samples, last, name
    )
    state = run([kv[None], kv_core[None]], None, (0, 1), False, "attend_near")
    ys, state, w_y, wz_y = hold((ys, state, w, w_z))
    w_up, w_down = over_sample(w_y, YUP), over_sample(w_y, YDOWN)
    wz_up, wz_down = over_sample(wz_y, YUP), over_sample(wz_y, YDOWN)
    rest = [jnp.concatenate([kv_z[None]] + ys, axis=0)]
    rest_core = [over_sample(rest[0], CORE)]
    state = run(rest, state, (0, 1), False, "attend_far")
    state, w_up, w_down = hold((state, w_up, w_down))
    half_lines = w.shape[0] // 2
    far_up = over_sample(w_up[:half_lines], YUP)
    far_down = over_sample(w_down[half_lines:], YDOWN)
    own = run(rest_core, state, (0,), True, "attend_own")
    own_core = over_sample(own, CORE)
    state, own = hold((state, own))
    partner = run(rest_core, state, (1,), True, "attend_partner")
    partner_core = over_sample(partner, CORE)
    partner, far_up, far_down = hold((partner, far_up, far_down))
    w_far = jnp.concatenate([far_up, far_down], axis=0)
    wz_far = over_sample(w_far, ZLO)

    rows = [a.reshape(8, 64, width) for a in (own, partner, partner_core, own_core)]
    early, after = sum_over_head(place, [w, w_z, w_up, w_down], rows, "_early")
    w_late, _ = hold(([w_far, wz_far, wz_up, wz_down], after))
    late, _ = sum_over_head(place, w_late, rows, "_late")

    got = [over_sample(early, CORE), over_sample(late, CORE)]
    return finish(place, [early, late], got, out_weight.shape[1])[None]


def solution(mesh):
    placed = (
        P("sample", None, "head"),
        P("sample", None, "head"),
        P("sample", None, "head"),
        P("sample", "head"),
        P("sample", "head"),
        P(),
        P("head", "sample"),
    )
    return jax.shard_map(
        per_device, mesh=mesh, in_specs=placed, out_specs=P("sample", "head", None), check_vma=False
    )
```

```python
import functools
import math

import jax
import jax.numpy as jnp
from jax import lax
from jax.experimental import pallas as pl
from jax.experimental.pallas import tpu as pltpu
from jax.sharding import PartitionSpec as P

HD = 128
HEADS = 4
TILE = 256
SCALE = HD ** (-0.5) * math.log2(math.e)
BF = jnp.bfloat16
F32 = jnp.float32
NT = (((1,), (1,)), ((), ()))


def sample_pairs(to):
    place = lambda z, y, c: (z * 4 + y) * 2 + c
    return [
        (place(z, y, c), place(*to(z, y, c)))
        for z in range(2) for y in range(4) for c in range(2)
    ]


def head_pairs(to):
    pairs = []
    for x in range(4):
        for z in range(2):
            tx, tz = to(x, z)
            pairs.append((x * 2 + z, tx * 2 + tz))
    return pairs


CORE = sample_pairs(lambda z, y, c: (z, y, 1 - c))
ZLO = sample_pairs(lambda z, y, c: (1 - z, y, c))
YUP = sample_pairs(lambda z, y, c: (z, (y + 1) % 4, c))
YDOWN = sample_pairs(lambda z, y, c: (z, (y + 3) % 4, c))
YFAR = sample_pairs(lambda z, y, c: (z, (y + 2) % 4, c))
XUP = head_pairs(lambda x, z: ((x + 1) % 4, z))
XDOWN = head_pairs(lambda x, z: ((x + 3) % 4, z))
XFAR = head_pairs(lambda x, z: ((x + 2) % 4, z))
ZHI = head_pairs(lambda x, z: (x, 1 - z))


def over_sample(value, pairs):
    return lax.ppermute(value, "sample", pairs)


def over_head(value, pairs):
    return lax.ppermute(value, "head", pairs)


X, Z_HI, CORE_AT, Y, Z_LO, LENGTH = range(6)


def attend_kernel(counts, samples, first, last, place_ref, q_own_ref, q_got_ref, *refs):
    refs = list(refs)
    suffix_refs = [refs.pop(0) for _ in range(4)] if first else None
    kv_refs = [refs.pop(0) for _ in counts]
    acc_in, stat_in = (None, None) if first else (refs.pop(0), refs.pop(0))
    if last:
        out_ref = refs.pop(0)
    else:
        acc_out, stat_out = refs.pop(0), refs.pop(0)
    keys_ref, values_ref = refs.pop(0), refs.pop(0)
    step, tile = pl.program_id(0), pl.program_id(1)
    sample = samples[0] + step
    rows_total = keys_ref.shape[0]

    @pl.when((step == 0) & (tile == 0))
    def _():
        at = 0
        for kv_ref, count in zip(kv_refs, counts):
            for b in range(count):
                block = kv_ref[b]
                rows = block.shape[0]
                keys_ref[at:at + rows] = block[:, :HD]
                values_ref[at:at + rows, :HD] = block[:, HD:]
                at += rows
        values_ref[:, HD:] = jnp.ones((rows_total, HD), BF)

    length = place_ref[LENGTH + sample]
    live = tile * TILE < length

    def pick(own, got):
        if len(samples) == 1:
            return got if samples[0] else own
        return jnp.where(sample == 0, own, got)

    def fold(state, scores, values):
        top = jnp.max(scores, axis=1, keepdims=True)
        if state is None:
            weights = jnp.exp2(scores - top)
            return top, jnp.dot(weights.astype(BF), values, preferred_element_type=F32)
        old, acc = state
        top = jnp.maximum(old, top)
        weights = jnp.exp2(scores - top)
        part = jnp.dot(weights.astype(BF), values, preferred_element_type=F32)
        return top, acc * jnp.exp2(old - top) + part

    def body(tile_static):
        for h in range(HEADS):
            cols = slice(h * HD, (h + 1) * HD)
            q = pick(q_own_ref[:, cols].astype(F32), q_got_ref[:, cols].astype(F32))
            q = (q * SCALE).astype(BF)
            state = None
            if first:
                row = lax.broadcasted_iota(jnp.int32, (TILE, TILE), 0)
                col = lax.broadcasted_iota(jnp.int32, (TILE, TILE), 1)
                for t in range(tile_static, -1, -1):
                    lines = slice(t * TILE, (t + 1) * TILE)
                    keys, values = (
                        pick(suffix_refs[i][lines], suffix_refs[i + 2][lines]) for i in (0, 1)
                    )
                    scores = lax.dot_general(q, keys, NT, preferred_element_type=F32)
                    if t == tile_static:
                        scores = jnp.where(col <= row, scores, -1e30)
                    values = jnp.concatenate([values, jnp.ones((TILE, HD), BF)], 1)
                    state = fold(state, scores, values)
            at = 0
            size = TILE if first else rows_total
            while at < rows_total:
                scores = lax.dot_general(q, keys_ref[at:at + size], NT, preferred_element_type=F32)
                state = fold(state, scores, values_ref[at:at + size])
                at += size
            top, acc = state
            num, den = acc[:, :HD], acc[:, HD:]
            if not first:
                top = jnp.broadcast_to(top, (TILE, HD))
                old = jnp.broadcast_to(stat_in[:, h:h + 1], (TILE, HD))
                total = jnp.broadcast_to(stat_in[:, HEADS + h:HEADS + h + 1], (TILE, HD))
                new = jnp.maximum(old, top)
                keep, add = jnp.exp2(old - new), jnp.exp2(top - new)
                num = acc_in[:, cols] * keep + num * add
                den = total * keep + den * add
                top = new[:, :1]
            if last:
                row = tile * TILE + lax.broadcasted_iota(jnp.int32, (TILE, HD), 0)
                out_ref[:, cols] = jnp.where(row < length, num / den, 0.0).astype(BF)
            else:
                acc_out[:, cols] = num
                stat_out[:, h:h + 1] = top
                stat_out[:, HEADS + h:HEADS + h + 1] = den[:, :1]

    if first:
        for t in range(2):
            pl.when(live & (tile == t))(functools.partial(body, t))
    else:
        pl.when(live)(functools.partial(body, 0))

    if last:
        @pl.when(jnp.logical_not(live))
        def _():
            out_ref[...] = jnp.zeros_like(out_ref)


def attend(place, q_own, q_got, suffixes, kvs, state, samples, last, name):
    first = state is None
    rows, width = q_got.shape[0], q_got.shape[1] // 2
    counts = [kv.shape[0] for kv in kvs]
    keys_total = sum(kv.shape[0] * kv.shape[1] for kv in kvs)
    tiled = lambda w, base: pl.BlockSpec((None, TILE, w), lambda s, t, p: (base + s, t, 0))
    whole = lambda a: pl.BlockSpec(a.shape, lambda s, t, p: (0,) * a.ndim)
    in_specs = [
        pl.BlockSpec((TILE, width), lambda s, t, p: (t, p[CORE_AT])),
        pl.BlockSpec((TILE, width), lambda s, t, p: (t, p[CORE_AT])),
    ]
    args = [q_own, q_got]
    for array in ([*suffixes] if first else []) + kvs:
        in_specs.append(whole(array))
        args.append(array)
    if not first:
        in_specs += [tiled(width, samples[0]), tiled(HD, samples[0])]
        args += list(state)
    count = len(samples)
    if last:
        out_specs = tiled(width, 0)
        out_shape = jax.ShapeDtypeStruct((count, rows, width), BF)
    else:
        out_specs = [tiled(width, 0), tiled(HD, 0)]
        out_shape = [
            jax.ShapeDtypeStruct((count, rows, width), F32),
            jax.ShapeDtypeStruct((count, rows, HD), F32),
        ]
    keys_seen = keys_total + (rows // 2 if first else 0)
    return pl.pallas_call(
        functools.partial(attend_kernel, counts, samples, first, last),
        grid_spec=pltpu.PrefetchScalarGridSpec(
            num_scalar_prefetch=1,
            grid=(count, rows // TILE),
            in_specs=in_specs,
            out_specs=out_specs,
            scratch_shapes=[
                pltpu.VMEM((keys_total, HD), BF),
                pltpu.VMEM((keys_total, 2 * HD), BF),
            ],
        ),
        out_shape=out_shape,
        name=name,
        cost_estimate=pl.CostEstimate(
            flops=count * rows * HEADS * keys_seen * HD * 32,
            bytes_accessed=4 * count * 2**20,
            transcendentals=count * rows * HEADS * keys_seen,
        ),
        compiler_params=pltpu.CompilerParams(vmem_limit_bytes=48 * 2**20),
    )(place, *args)


OTHER, OWN = False, True
FEATURES = 320


def project_kernel(tiles, count, spans, place_ref, *refs):
    weight_refs = refs[:2 * tiles]
    rows_refs = refs[2 * tiles:2 * tiles + 4 * count]
    add_refs, out_ref, held_ref = refs[2 * tiles + 4 * count:-2], refs[-2], refs[-1]
    tile = pl.program_id(0)
    own = jnp.concatenate([r[...] for b in range(count) for r in rows_refs[4 * b:4 * b + 2]], axis=0)
    other = jnp.concatenate(
        [r[...] for b in range(count) for r in rows_refs[4 * b + 2:4 * b + 4]], axis=0
    )

    def bring(at):
        held_ref[0] = weight_refs[2 * at][...]
        held_ref[1] = weight_refs[2 * at + 1][...]

    for at in range(tiles):
        pl.when(tile == at)(functools.partial(bring, at))
    acc = lax.dot_general(held_ref[0], own, NT, preferred_element_type=F32)
    acc += lax.dot_general(held_ref[1], other, NT, preferred_element_type=F32)
    for ref, (start, length) in zip(add_refs, spans):
        here = (tile >= start) & (tile < start + length)
        acc += ref[...].astype(F32) if length == tiles else jnp.where(here, ref[...].astype(F32), 0.0)
    out_ref[...] = acc.astype(out_ref.dtype)


def project(place, weights, rows, blocks, adds, name, kind=BF):
    tiles = len(weights)
    size = FEATURES
    part, depth = rows[0].shape[1:]
    lanes = 2 * part * len(blocks)

    def rows_spec(step, own):
        def index(i, p):
            z = p[Z_HI] if own else 1 - p[Z_HI]
            return (2 * lax.rem(p[X] + step, 4) + z, 0, 0)

        return pl.BlockSpec((None, part, depth), index)

    def add_spec(lane, start, count):
        return pl.BlockSpec(
            (size, lanes), lambda i, p: (jnp.clip(i - start, 0, count - 1), lane)
        )

    in_specs, args = [], []
    for weight, at in weights:
        in_specs.append(pl.BlockSpec((size, depth), lambda i, p, at=at: (at, p[CORE_AT])))
        in_specs.append(pl.BlockSpec((size, depth), lambda i, p, at=at: (at, 1 - p[CORE_AT])))
        args += [weight, weight]
    for block in blocks:
        in_specs += [rows_spec(*block)] * 4
        args += rows
    for array, lane, start, count in adds:
        in_specs.append(add_spec(lane, start, count))
        args.append(array)
    return pl.pallas_call(
        functools.partial(project_kernel, tiles, len(blocks), [a[2:] for a in adds]),
        grid_spec=pltpu.PrefetchScalarGridSpec(
            num_scalar_prefetch=1,
            grid=(tiles,),
            in_specs=in_specs,
            out_specs=pl.BlockSpec((size, lanes), lambda i, p: (i, 0)),
            scratch_shapes=[pltpu.VMEM((2, size, depth), BF)],
        ),
        out_shape=jax.ShapeDtypeStruct((tiles * size, lanes), kind),
        name=name,
        cost_estimate=pl.CostEstimate(
            flops=4 * tiles * size * lanes * depth,
            bytes_accessed=4 * tiles * size * depth + 2 * tiles * size * lanes,
            transcendentals=0,
        ),
        compiler_params=pltpu.CompilerParams(vmem_limit_bytes=32 * 2**20),
    )(place, *args)


def gather_kernel(count, base_ref, *refs):
    out_ref = refs[-1]
    halves, whole = refs[:-1 - count], refs[-1 - count:-1]
    lines = base_ref.shape[0] // 2
    for half in range(2):
        at = slice(half * lines, (half + 1) * lines)
        acc = base_ref[at]
        for ref in halves[half::2]:
            acc += ref[...].astype(F32)
        for ref in whole:
            acc += ref[at].astype(F32)
        out_ref[at] = acc.astype(BF)


def gather(base, lane, halves, whole, name):
    lines = base.shape[0]
    halves = [array for pair in halves for array in pair]
    spec = lambda size, at: pl.BlockSpec((size, 128), lambda i: (0, at))
    return pl.pallas_call(
        functools.partial(gather_kernel, len(whole)),
        grid=(1,),
        in_specs=[spec(lines, lane)] + [spec(lines // 2, lane)] * len(halves)
        + [spec(lines, 0)] * len(whole),
        out_specs=spec(lines, 0),
        out_shape=jax.ShapeDtypeStruct((lines, 128), BF),
        name=name,
        cost_estimate=pl.CostEstimate(
            flops=6 * lines * 128, bytes_accessed=20 * lines * 128, transcendentals=0
        ),
        compiler_params=pltpu.CompilerParams(vmem_limit_bytes=32 * 2**20),
    )(base, *halves, *whole)


def sum_over_head(place, weights, rows, tag, beside=()):
    run = lambda w, blocks, adds, name, kind=BF: project(
        place, w, rows, blocks, adds, name + tag, kind
    )
    both = lambda step: [(step, OTHER), (step, OWN)]
    n = len(weights) // 2
    top, low = weights[:n], weights[n:]
    via_up = over_head(run(top, both(2), [], "far_top"), XUP)
    via_down = over_head(run(low, both(2), [], "far_low"), XDOWN)
    via_up, via_down, beside = lax.optimization_barrier((via_up, via_down, beside))
    below_low = over_head(run(low, both(1), [], "up_low"), XUP)
    above_top = over_head(run(top, both(3), [], "down_top"), XDOWN)
    below_top = over_head(run(top, both(1), [(via_up, 0, 0, n)], "up_top"), XUP)
    above_low = over_head(run(low, both(3), [(via_down, 0, 0, n)], "down_low"), XDOWN)
    own = run(weights, both(0), [], "own", F32)
    arrived = [(below_top, below_low), (above_top, above_low)]
    from_z = over_head(gather(own, 0, arrived, [], "give" + tag), ZHI)
    return from_z, lambda from_z: gather(own, 1, arrived, [from_z], "sum" + tag), beside


def give_z_first(place, weights, rows, tag):
    return project(place, weights, rows, [(step, OTHER) for step in range(4)], [], "give" + tag)


def sum_z_first(place, weights, rows, got, tag):
    part = lambda step, name, kind: project(
        place, weights, rows, [(step, OWN)], [(got, step, 0, len(weights))], name + tag, kind
    )
    sends = [(part(step, name, BF), to) for step, name, to in FAR_UP_DOWN]
    return sends, part(0, "own", F32)


FAR_UP_DOWN = ((2, "far", XFAR), (1, "up", XUP), (3, "down", XDOWN))


EARLY_FROM = ((0, 0), (1, 0), (0, 3), (1, 3), (0, 1), (1, 1))
LATE_FROM = ((0, 2), (1, 2))


def finish_kernel(place_ref, from_ref, own_ref, got_ref, *refs):
    out_ref = refs[-1]
    lane = lax.broadcasted_iota(jnp.int32, (64, 128), 1)
    row = lax.broadcasted_iota(jnp.int32, (64, 128), 0)
    turn = lambda array, at: lax.dot_general(
        jnp.where(lane == row + at, 1.0, 0.0).astype(BF), array, NT, preferred_element_type=F32
    )
    own, got = turn(own_ref[...], 0), turn(got_ref[...], 64)
    first = place_ref[CORE_AT] == 0
    even, odd = jnp.where(first, own, got), jnp.where(first, got, own)
    out_ref[...] = jnp.concatenate([even, odd], axis=1).astype(BF)


def finish(place, own, got, chips, out, name):
    wide = 2 * FEATURES
    offsets = jnp.array([d for chip in chips for d in chip], jnp.int32)

    def to(i, p, f):
        z = lax.rem(f[2 * i] + p[Z_LO], 2)
        return (0, z * 4 + lax.rem(f[2 * i + 1] + p[Y], 4))

    part = pl.BlockSpec((FEATURES, 128), lambda i, p, f: (i, 0))
    return pl.pallas_call(
        finish_kernel,
        grid_spec=pltpu.PrefetchScalarGridSpec(
            num_scalar_prefetch=2,
            grid=(len(chips),),
            in_specs=[part, part] + [pl.BlockSpec(memory_space=pl.ANY)] * len(out),
            out_specs=pl.BlockSpec((64, wide), to),
        ),
        out_shape=jax.ShapeDtypeStruct((64, 8 * wide), BF),
        input_output_aliases={4: 0} if out else {},
        name=name,
        cost_estimate=pl.CostEstimate(
            flops=len(chips) * 2 * 64 * 128 * wide,
            bytes_accessed=len(chips) * wide * 400,
            transcendentals=0,
        ),
        compiler_params=pltpu.CompilerParams(vmem_limit_bytes=32 * 2**20),
    )(place, offsets, own, got, *out)


def per_device(
    queries, suffix_keys, suffix_values, prefix_keys, prefix_values, lengths, out_weight
):
    hold = lax.optimization_barrier
    sample = lax.axis_index("sample")
    head = lax.axis_index("head")
    core = sample % 2
    width = queries.shape[2] // 2
    place = jnp.stack([
        head // 2, head % 2, core, (sample // 2) % 4, sample // 8,
        lengths[sample], lengths[sample + 1 - 2 * core],
    ]).astype(jnp.int32)

    kv = jnp.concatenate([prefix_keys, prefix_values], axis=1)
    kv_z = over_sample(kv, ZLO)
    q_own = queries[0]
    q_got = over_sample(q_own, CORE)
    suffix = [suffix_keys[0], suffix_values[0]]
    suffixes = suffix + [over_sample(a, CORE) for a in suffix]
    kv_core = over_sample(kv, CORE)
    w, kv_z = hold((out_weight.T, kv_z))
    w_z = over_sample(w, ZLO)
    near = jnp.stack([kv, kv_z])
    ys = [over_sample(near, to) for to in (YUP, YDOWN, YFAR)]

    run = lambda kvs, state, samples, last, name: attend(
        place, q_own, q_got, suffixes, kvs, state, samples, last, name
    )
    state = run([kv[None], kv_core[None]], None, (0, 1), False, "attend_near")
    ys, state, w_z = hold((ys, state, w_z))
    w_pair = jnp.concatenate([w, w_z], axis=0)
    w_up, w_down = over_sample(w_pair, YUP), over_sample(w_pair, YDOWN)
    rest = [jnp.concatenate([kv_z[None]] + ys, axis=0)]
    rest_core = [over_sample(rest[0], CORE)]
    state = run(rest, state, (0, 1), False, "attend_far")
    own = run(rest_core, state, (0,), True, "attend_own")
    own_core = over_sample(own, CORE)
    state, own = hold((state, own))
    partner = run(rest_core, state, (1,), True, "attend_partner")
    partner_core = over_sample(partner, CORE)
    partner, w_up, w_down = hold((partner, w_up, w_down))
    w_far = over_sample(w_up[:FEATURES], YUP)
    wz_far = over_sample(w_down[FEATURES:], YDOWN)

    rows = [a.reshape(8, 64, width) for a in (own, partner, partner_core, own_core)]
    w_early = [(w_pair, 0), (w_pair, 1), (w_up, 0), (w_up, 1), (w_down, 0), (w_down, 1)]
    w_late = [(w_far, 0), (wz_far, 0)]
    give_late = give_z_first(place, w_late, rows, "_late")
    from_z, finish_early, give_late = sum_over_head(place, w_early, rows, "_early", give_late)
    got = over_head(give_late, ZHI)
    sends, own = sum_z_first(place, w_late, rows, got, "_late")
    arrived = [over_head(part, to) for part, to in sends]
    from_z, arrived = hold((from_z, arrived))
    early = finish_early(from_z)
    late = gather(own, 0, [], arrived, "sum_late")

    out = finish(place, early, over_sample(early, CORE), EARLY_FROM, [], "finish_early")
    out = finish(place, late, over_sample(late, CORE), LATE_FROM, [out], "finish_late")
    return out[None]


def solution(mesh):
    placed = (
        P("sample", None, "head"),
        P("sample", None, "head"),
        P("sample", None, "head"),
        P("sample", "head"),
        P("sample", "head"),
        P(),
        P("head", "sample"),
    )
    return jax.shard_map(
        per_device, mesh=mesh, in_specs=placed, out_specs=P("sample", "head", None), check_vma=False
    )
```

```python
import functools
import math

import jax
import jax.numpy as jnp
from jax import lax
from jax.experimental import pallas as pl
from jax.experimental.pallas import tpu as pltpu
from jax.sharding import PartitionSpec as P

HD = 128
HEADS = 4
TILE = 256
SCALE = HD ** (-0.5) * math.log2(math.e)
BF = jnp.bfloat16
F32 = jnp.float32
NT = (((1,), (1,)), ((), ()))


def sample_pairs(to):
    place = lambda z, y, c: (z * 4 + y) * 2 + c
    return [
        (place(z, y, c), place(*to(z, y, c)))
        for z in range(2) for y in range(4) for c in range(2)
    ]


def head_pairs(to):
    pairs = []
    for x in range(4):
        for z in range(2):
            tx, tz = to(x, z)
            pairs.append((x * 2 + z, tx * 2 + tz))
    return pairs


CORE = sample_pairs(lambda z, y, c: (z, y, 1 - c))
ZLO = sample_pairs(lambda z, y, c: (1 - z, y, c))
YUP = sample_pairs(lambda z, y, c: (z, (y + 1) % 4, c))
YDOWN = sample_pairs(lambda z, y, c: (z, (y + 3) % 4, c))
YFAR = sample_pairs(lambda z, y, c: (z, (y + 2) % 4, c))
XUP = head_pairs(lambda x, z: ((x + 1) % 4, z))
XDOWN = head_pairs(lambda x, z: ((x + 3) % 4, z))
XFAR = head_pairs(lambda x, z: ((x + 2) % 4, z))
ZHI = head_pairs(lambda x, z: (x, 1 - z))


def over_sample(value, pairs):
    return lax.ppermute(value, "sample", pairs)


def over_head(value, pairs):
    return lax.ppermute(value, "head", pairs)


X, Z_HI, CORE_AT, Y, Z_LO, LENGTH = range(6)


def attend_kernel(counts, samples, first, last, place_ref, q_own_ref, q_got_ref, *refs):
    refs = list(refs)
    suffix_refs = [refs.pop(0) for _ in range(4)] if first else None
    kv_refs = [refs.pop(0) for _ in counts]
    acc_in, stat_in = (None, None) if first else (refs.pop(0), refs.pop(0))
    if last:
        out_ref = refs.pop(0)
    else:
        acc_out, stat_out = refs.pop(0), refs.pop(0)
    keys_ref, values_ref = refs.pop(0), refs.pop(0)
    step, tile = pl.program_id(0), pl.program_id(1)
    sample = samples[0] + step
    rows_total = keys_ref.shape[0]

    @pl.when((step == 0) & (tile == 0))
    def _():
        at = 0
        for kv_ref, count in zip(kv_refs, counts):
            for b in range(count):
                block = kv_ref[b]
                rows = block.shape[0]
                keys_ref[at:at + rows] = block[:, :HD]
                values_ref[at:at + rows, :HD] = block[:, HD:]
                at += rows
        values_ref[:, HD:] = jnp.ones((rows_total, HD), BF)

    length = place_ref[LENGTH + sample]
    live = tile * TILE < length

    def pick(own, got):
        if len(samples) == 1:
            return got if samples[0] else own
        return jnp.where(sample == 0, own, got)

    def fold(state, scores, values):
        top = jnp.max(scores, axis=1, keepdims=True)
        if state is None:
            weights = jnp.exp2(scores - top)
            return top, jnp.dot(weights.astype(BF), values, preferred_element_type=F32)
        old, acc = state
        top = jnp.maximum(old, top)
        weights = jnp.exp2(scores - top)
        part = jnp.dot(weights.astype(BF), values, preferred_element_type=F32)
        return top, acc * jnp.exp2(old - top) + part

    def body(tile_static):
        for h in range(HEADS):
            cols = slice(h * HD, (h + 1) * HD)
            q = pick(q_own_ref[:, cols].astype(F32), q_got_ref[:, cols].astype(F32))
            q = (q * SCALE).astype(BF)
            state = None
            if first:
                row = lax.broadcasted_iota(jnp.int32, (TILE, TILE), 0)
                col = lax.broadcasted_iota(jnp.int32, (TILE, TILE), 1)
                for t in range(tile_static, -1, -1):
                    lines = slice(t * TILE, (t + 1) * TILE)
                    keys, values = (
                        pick(suffix_refs[i][lines], suffix_refs[i + 2][lines]) for i in (0, 1)
                    )
                    scores = lax.dot_general(q, keys, NT, preferred_element_type=F32)
                    if t == tile_static:
                        scores = jnp.where(col <= row, scores, -1e30)
                    values = jnp.concatenate([values, jnp.ones((TILE, HD), BF)], 1)
                    state = fold(state, scores, values)
            at = 0
            size = TILE if first else rows_total
            while at < rows_total:
                scores = lax.dot_general(q, keys_ref[at:at + size], NT, preferred_element_type=F32)
                state = fold(state, scores, values_ref[at:at + size])
                at += size
            top, acc = state
            num, den = acc[:, :HD], acc[:, HD:]
            if not first:
                top = jnp.broadcast_to(top, (TILE, HD))
                old = jnp.broadcast_to(stat_in[:, h:h + 1], (TILE, HD))
                total = jnp.broadcast_to(stat_in[:, HEADS + h:HEADS + h + 1], (TILE, HD))
                new = jnp.maximum(old, top)
                keep, add = jnp.exp2(old - new), jnp.exp2(top - new)
                num = acc_in[:, cols] * keep + num * add
                den = total * keep + den * add
                top = new[:, :1]
            if last:
                row = tile * TILE + lax.broadcasted_iota(jnp.int32, (TILE, HD), 0)
                out_ref[:, cols] = jnp.where(row < length, num / den, 0.0).astype(BF)
            else:
                acc_out[:, cols] = num
                stat_out[:, h:h + 1] = top
                stat_out[:, HEADS + h:HEADS + h + 1] = den[:, :1]

    if first:
        for t in range(2):
            pl.when(live & (tile == t))(functools.partial(body, t))
    else:
        pl.when(live)(functools.partial(body, 0))

    if last:
        @pl.when(jnp.logical_not(live))
        def _():
            out_ref[...] = jnp.zeros_like(out_ref)


def attend(place, q_own, q_got, suffixes, kvs, state, samples, last, name):
    first = state is None
    rows, width = q_got.shape[0], q_got.shape[1] // 2
    counts = [kv.shape[0] for kv in kvs]
    keys_total = sum(kv.shape[0] * kv.shape[1] for kv in kvs)
    tiled = lambda w, base: pl.BlockSpec((None, TILE, w), lambda s, t, p: (base + s, t, 0))
    whole = lambda a: pl.BlockSpec(a.shape, lambda s, t, p: (0,) * a.ndim)
    in_specs = [
        pl.BlockSpec((TILE, width), lambda s, t, p: (t, p[CORE_AT])),
        pl.BlockSpec((TILE, width), lambda s, t, p: (t, p[CORE_AT])),
    ]
    args = [q_own, q_got]
    for array in ([*suffixes] if first else []) + kvs:
        in_specs.append(whole(array))
        args.append(array)
    if not first:
        in_specs += [tiled(width, samples[0]), tiled(HD, samples[0])]
        args += list(state)
    count = len(samples)
    if last:
        out_specs = tiled(width, 0)
        out_shape = jax.ShapeDtypeStruct((count, rows, width), BF)
    else:
        out_specs = [tiled(width, 0), tiled(HD, 0)]
        out_shape = [
            jax.ShapeDtypeStruct((count, rows, width), F32),
            jax.ShapeDtypeStruct((count, rows, HD), F32),
        ]
    keys_seen = keys_total + (rows // 2 if first else 0)
    return pl.pallas_call(
        functools.partial(attend_kernel, counts, samples, first, last),
        grid_spec=pltpu.PrefetchScalarGridSpec(
            num_scalar_prefetch=1,
            grid=(count, rows // TILE),
            in_specs=in_specs,
            out_specs=out_specs,
            scratch_shapes=[
                pltpu.VMEM((keys_total, HD), BF),
                pltpu.VMEM((keys_total, 2 * HD), BF),
            ],
        ),
        out_shape=out_shape,
        name=name,
        cost_estimate=pl.CostEstimate(
            flops=count * rows * HEADS * keys_seen * HD * 32,
            bytes_accessed=4 * count * 2**20,
            transcendentals=count * rows * HEADS * keys_seen,
        ),
        compiler_params=pltpu.CompilerParams(vmem_limit_bytes=48 * 2**20),
    )(place, *args)


OTHER, OWN = False, True
FEATURES = 320


def project_kernel(tiles, count, spans, outs, place_ref, *refs):
    weight_refs = refs[:2 * tiles]
    rows_refs = refs[2 * tiles:2 * tiles + 4 * count]
    add_refs = refs[2 * tiles + 4 * count:-1 - outs]
    out_refs, held_ref = refs[-1 - outs:-1], refs[-1]
    tile = pl.program_id(0)
    own = jnp.concatenate([r[...] for b in range(count) for r in rows_refs[4 * b:4 * b + 2]], axis=0)
    other = jnp.concatenate(
        [r[...] for b in range(count) for r in rows_refs[4 * b + 2:4 * b + 4]], axis=0
    )

    def bring(at):
        held_ref[0] = weight_refs[2 * at][...]
        held_ref[1] = weight_refs[2 * at + 1][...]

    for at in range(tiles):
        pl.when(tile == at)(functools.partial(bring, at))
    acc = lax.dot_general(held_ref[0], own, NT, preferred_element_type=F32)
    acc += lax.dot_general(held_ref[1], other, NT, preferred_element_type=F32)
    for ref, (start, length) in zip(add_refs, spans):
        here = (tile >= start) & (tile < start + length)
        acc += ref[...].astype(F32) if length == tiles else jnp.where(here, ref[...].astype(F32), 0.0)
    lanes = acc.shape[1] // outs
    for k, out_ref in enumerate(out_refs):
        out_ref[...] = acc[:, k * lanes:(k + 1) * lanes].astype(out_ref.dtype)


def project(place, weights, rows, blocks, adds, name, *kinds):
    tiles = len(weights)
    size = FEATURES
    kinds = kinds or (BF,)
    part, depth = rows[0].shape[1:]
    lanes = 2 * part * len(blocks)

    def rows_spec(step, own):
        def index(i, p):
            z = p[Z_HI] if own else 1 - p[Z_HI]
            return (2 * lax.rem(p[X] + step, 4) + z, 0, 0)

        return pl.BlockSpec((None, part, depth), index)

    def add_spec(lane, start, count):
        return pl.BlockSpec(
            (size, lanes), lambda i, p: (jnp.clip(i - start, 0, count - 1), lane)
        )

    in_specs, args = [], []
    for weight, at in weights:
        in_specs.append(pl.BlockSpec((size, depth), lambda i, p, at=at: (at, p[CORE_AT])))
        in_specs.append(pl.BlockSpec((size, depth), lambda i, p, at=at: (at, 1 - p[CORE_AT])))
        args += [weight, weight]
    for block in blocks:
        in_specs += [rows_spec(*block)] * 4
        args += rows
    for array, lane, start, count in adds:
        in_specs.append(add_spec(lane, start, count))
        args.append(array)
    wide = lanes // len(kinds)
    results = pl.pallas_call(
        functools.partial(project_kernel, tiles, len(blocks), [a[2:] for a in adds], len(kinds)),
        grid_spec=pltpu.PrefetchScalarGridSpec(
            num_scalar_prefetch=1,
            grid=(tiles,),
            in_specs=in_specs,
            out_specs=[pl.BlockSpec((size, wide), lambda i, p: (i, 0))] * len(kinds),
            scratch_shapes=[pltpu.VMEM((2, size, depth), BF)],
        ),
        out_shape=[jax.ShapeDtypeStruct((tiles * size, wide), kind) for kind in kinds],
        name=name,
        cost_estimate=pl.CostEstimate(
            flops=4 * tiles * size * lanes * depth,
            bytes_accessed=4 * tiles * size * depth + 2 * tiles * size * lanes,
            transcendentals=0,
        ),
        compiler_params=pltpu.CompilerParams(vmem_limit_bytes=32 * 2**20),
    )(place, *args)
    return results if len(kinds) > 1 else results[0]


def gather_kernel(count, base_ref, *refs):
    out_ref = refs[-1]
    halves, whole = refs[:-1 - count], refs[-1 - count:-1]
    lines = base_ref.shape[0] // 2
    for half in range(2):
        at = slice(half * lines, (half + 1) * lines)
        acc = base_ref[at]
        for ref in halves[half::2]:
            acc += ref[...].astype(F32)
        for ref in whole:
            acc += ref[at].astype(F32)
        out_ref[at] = acc.astype(BF)


def gather(base, lane, halves, whole, name):
    lines = base.shape[0]
    halves = [array for pair in halves for array in pair]
    spec = lambda size, at: pl.BlockSpec((size, 128), lambda i: (0, at))
    return pl.pallas_call(
        functools.partial(gather_kernel, len(whole)),
        grid=(1,),
        in_specs=[spec(lines, lane)] + [spec(lines // 2, lane)] * len(halves)
        + [spec(lines, 0)] * len(whole),
        out_specs=spec(lines, 0),
        out_shape=jax.ShapeDtypeStruct((lines, 128), BF),
        name=name,
        cost_estimate=pl.CostEstimate(
            flops=6 * lines * 128, bytes_accessed=20 * lines * 128, transcendentals=0
        ),
        compiler_params=pltpu.CompilerParams(vmem_limit_bytes=32 * 2**20),
    )(base, *halves, *whole)


def sum_over_head(place, weights, rows, tag, beside=()):
    run = lambda w, blocks, adds, name, *kinds: project(
        place, w, rows, blocks, adds, name + tag, *kinds
    )
    both = lambda step: [(step, OTHER), (step, OWN)]
    n = len(weights) // 2
    top, low = weights[:n], weights[n:]
    via_up = over_head(run(top, both(2), [], "far_top"), XUP)
    via_down = over_head(run(low, both(2), [], "far_low"), XDOWN)
    via_up, via_down, beside = lax.optimization_barrier((via_up, via_down, beside))
    below_low = over_head(run(low, both(1), [], "up_low"), XUP)
    above_top = over_head(run(top, both(3), [], "down_top"), XDOWN)
    below_top = over_head(run(top, both(1), [(via_up, 0, 0, n)], "up_top"), XUP)
    above_low = over_head(run(low, both(3), [(via_down, 0, 0, n)], "down_low"), XDOWN)
    own = run(weights, both(0), [], "own", F32)
    arrived = [(below_top, below_low), (above_top, above_low)]
    from_z = over_head(gather(own, 0, arrived, [], "give" + tag), ZHI)
    return from_z, lambda from_z: gather(own, 1, arrived, [from_z], "sum" + tag), beside


def give_z_first(place, weights, rows, tag):
    return project(place, weights, rows, [(step, OTHER) for step in range(4)], [], "give" + tag)


def sum_z_first(place, weights, rows, got, tag):
    steps = [(step, OWN) for step in range(4)]
    adds = [(got, 0, 0, len(weights))]
    return project(place, weights, rows, steps, adds, "steps" + tag, F32, BF, BF, BF)


EARLY_FROM = ((0, 0), (1, 0), (0, 3), (1, 3), (0, 1), (1, 1))
LATE_FROM = ((0, 2), (1, 2))


def finish_kernel(place_ref, from_ref, own_ref, got_ref, *refs):
    out_ref = refs[-1]
    lane = lax.broadcasted_iota(jnp.int32, (64, 128), 1)
    row = lax.broadcasted_iota(jnp.int32, (64, 128), 0)
    turn = lambda array, at: lax.dot_general(
        jnp.where(lane == row + at, 1.0, 0.0).astype(BF), array, NT, preferred_element_type=F32
    )
    own, got = turn(own_ref[...], 0), turn(got_ref[...], 64)
    first = place_ref[CORE_AT] == 0
    even, odd = jnp.where(first, own, got), jnp.where(first, got, own)
    out_ref[...] = jnp.concatenate([even, odd], axis=1).astype(BF)


def finish(place, own, got, chips, out, name):
    wide = 2 * FEATURES
    offsets = jnp.array([d for chip in chips for d in chip], jnp.int32)

    def to(i, p, f):
        z = lax.rem(f[2 * i] + p[Z_LO], 2)
        return (0, z * 4 + lax.rem(f[2 * i + 1] + p[Y], 4))

    part = pl.BlockSpec((FEATURES, 128), lambda i, p, f: (i, 0))
    return pl.pallas_call(
        finish_kernel,
        grid_spec=pltpu.PrefetchScalarGridSpec(
            num_scalar_prefetch=2,
            grid=(len(chips),),
            in_specs=[part, part] + [pl.BlockSpec(memory_space=pl.ANY)] * len(out),
            out_specs=pl.BlockSpec((64, wide), to),
        ),
        out_shape=jax.ShapeDtypeStruct((64, 8 * wide), BF),
        input_output_aliases={4: 0} if out else {},
        name=name,
        cost_estimate=pl.CostEstimate(
            flops=len(chips) * 2 * 64 * 128 * wide,
            bytes_accessed=len(chips) * wide * 400,
            transcendentals=0,
        ),
        compiler_params=pltpu.CompilerParams(vmem_limit_bytes=32 * 2**20),
    )(place, offsets, own, got, *out)


def per_device(
    queries, suffix_keys, suffix_values, prefix_keys, prefix_values, lengths, out_weight
):
    hold = lax.optimization_barrier
    sample = lax.axis_index("sample")
    head = lax.axis_index("head")
    core = sample % 2
    width = queries.shape[2] // 2
    place = jnp.stack([
        head // 2, head % 2, core, (sample // 2) % 4, sample // 8,
        lengths[sample], lengths[sample + 1 - 2 * core],
    ]).astype(jnp.int32)

    kv = jnp.concatenate([prefix_keys, prefix_values], axis=1)
    kv_z = over_sample(kv, ZLO)
    q_own = queries[0]
    q_got = over_sample(q_own, CORE)
    suffix = [suffix_keys[0], suffix_values[0]]
    suffixes = suffix + [over_sample(a, CORE) for a in suffix]
    kv_core = over_sample(kv, CORE)
    w, kv = hold((out_weight.T, kv))
    w_z = over_sample(w, ZLO)
    near = jnp.stack([kv, kv_z])
    ys = [over_sample(near, to) for to in (YUP, YDOWN, YFAR)]

    run = lambda kvs, state, samples, last, name: attend(
        place, q_own, q_got, suffixes, kvs, state, samples, last, name
    )
    state = run([kv[None], kv_core[None]], None, (0, 1), False, "attend_near")
    ys, state, w_z = hold((ys, state, w_z))
    w_pair = jnp.concatenate([w, w_z], axis=0)
    w_up, w_down = over_sample(w_pair, YUP), over_sample(w_pair, YDOWN)
    rest = [jnp.concatenate([kv_z[None]] + ys, axis=0)]
    rest_core = [over_sample(rest[0], CORE)]
    state = run(rest, state, (0, 1), False, "attend_far")
    own = run(rest_core, state, (0,), True, "attend_own")
    own_core = over_sample(own, CORE)
    state, own = hold((state, own))
    partner = run(rest_core, state, (1,), True, "attend_partner")
    partner_core = over_sample(partner, CORE)
    partner, w_up, w_down = hold((partner, w_up, w_down))
    w_far = over_sample(w_up[:FEATURES], YUP)
    wz_far = over_sample(w_down[FEATURES:], YDOWN)

    rows = [a.reshape(8, 64, width) for a in (own, partner, partner_core, own_core)]
    w_early = [(w_pair, 0), (w_pair, 1), (w_up, 0), (w_up, 1), (w_down, 0), (w_down, 1)]
    w_late = [(w_far, 0), (wz_far, 0)]
    give_late = give_z_first(place, w_late, rows, "_late")
    from_z, finish_early, give_late = sum_over_head(place, w_early, rows, "_early", give_late)
    got = over_head(give_late, ZHI)
    own, up, far, down = sum_z_first(place, w_late, rows, got, "_late")
    arrived = [over_head(far, XFAR), over_head(up, XUP), over_head(down, XDOWN)]
    from_z, arrived = hold((from_z, arrived))
    early = finish_early(from_z)
    late = gather(own, 0, [], arrived, "sum_late")

    out = finish(place, early, over_sample(early, CORE), EARLY_FROM, [], "finish_early")
    out = finish(place, late, over_sample(late, CORE), LATE_FROM, [out], "finish_late")
    return out[None]


def solution(mesh):
    placed = (
        P("sample", None, "head"),
        P("sample", None, "head"),
        P("sample", None, "head"),
        P("sample", "head"),
        P("sample", "head"),
        P(),
        P("head", "sample"),
    )
    return jax.shard_map(
        per_device, mesh=mesh, in_specs=placed, out_specs=P("sample", "head", None), check_vma=False
    )
```

```python
import functools
import math

import jax
import jax.numpy as jnp
from jax import lax
from jax.experimental import pallas as pl
from jax.experimental.pallas import tpu as pltpu
from jax.sharding import PartitionSpec as P

HD = 128
HEADS = 4
TILE = 256
SCALE = HD ** (-0.5) * math.log2(math.e)
BF = jnp.bfloat16
F32 = jnp.float32
NT = (((1,), (1,)), ((), ()))


def sample_pairs(to):
    place = lambda z, y, c: (z * 4 + y) * 2 + c
    return [
        (place(z, y, c), place(*to(z, y, c)))
        for z in range(2) for y in range(4) for c in range(2)
    ]


def head_pairs(to):
    pairs = []
    for x in range(4):
        for z in range(2):
            tx, tz = to(x, z)
            pairs.append((x * 2 + z, tx * 2 + tz))
    return pairs


CORE = sample_pairs(lambda z, y, c: (z, y, 1 - c))
ZLO = sample_pairs(lambda z, y, c: (1 - z, y, c))
YUP = sample_pairs(lambda z, y, c: (z, (y + 1) % 4, c))
YDOWN = sample_pairs(lambda z, y, c: (z, (y + 3) % 4, c))
YFAR = sample_pairs(lambda z, y, c: (z, (y + 2) % 4, c))
XUP = head_pairs(lambda x, z: ((x + 1) % 4, z))
XDOWN = head_pairs(lambda x, z: ((x + 3) % 4, z))
XFAR = head_pairs(lambda x, z: ((x + 2) % 4, z))
ZHI = head_pairs(lambda x, z: (x, 1 - z))


def over_sample(value, pairs):
    return lax.ppermute(value, "sample", pairs)


def over_head(value, pairs):
    return lax.ppermute(value, "head", pairs)


X, Z_HI, CORE_AT, Y, Z_LO, LENGTH = range(6)


def attend_kernel(counts, samples, first, last, place_ref, q_own_ref, q_got_ref, *refs):
    refs = list(refs)
    suffix_refs = [refs.pop(0) for _ in range(4)] if first else None
    kv_refs = [refs.pop(0) for _ in counts]
    acc_in, stat_in = (None, None) if first else (refs.pop(0), refs.pop(0))
    if last:
        out_ref = refs.pop(0)
    else:
        acc_out, stat_out = refs.pop(0), refs.pop(0)
    keys_ref, values_ref = refs.pop(0), refs.pop(0)
    step, tile = pl.program_id(0), pl.program_id(1)
    sample = samples[0] + step
    rows_total = keys_ref.shape[0]

    @pl.when((step == 0) & (tile == 0))
    def _():
        at = 0
        for kv_ref, count in zip(kv_refs, counts):
            for b in range(count):
                block = kv_ref[b]
                rows = block.shape[0]
                keys_ref[at:at + rows] = block[:, :HD]
                values_ref[at:at + rows, :HD] = block[:, HD:]
                at += rows
        values_ref[:, HD:] = jnp.ones((rows_total, HD), BF)

    length = place_ref[LENGTH + sample]
    live = tile * TILE < length

    def pick(own, got):
        if len(samples) == 1:
            return got if samples[0] else own
        return jnp.where(sample == 0, own, got)

    def fold(state, scores, values):
        top = jnp.max(scores, axis=1, keepdims=True)
        if state is None:
            weights = jnp.exp2((scores - top) * SCALE)
            return top, jnp.dot(weights.astype(BF), values, preferred_element_type=F32)
        old, acc = state
        top = jnp.maximum(old, top)
        weights = jnp.exp2((scores - top) * SCALE)
        part = jnp.dot(weights.astype(BF), values, preferred_element_type=F32)
        return top, acc * jnp.exp2((old - top) * SCALE) + part

    def body(tile_static):
        for h in range(HEADS):
            cols = slice(h * HD, (h + 1) * HD)
            q = pick(q_own_ref[:, cols], q_got_ref[:, cols])
            state = None
            if first:
                row = lax.broadcasted_iota(jnp.int32, (TILE, TILE), 0)
                col = lax.broadcasted_iota(jnp.int32, (TILE, TILE), 1)
                for t in range(tile_static, -1, -1):
                    lines = slice(t * TILE, (t + 1) * TILE)
                    keys, values = (
                        pick(suffix_refs[i][lines], suffix_refs[i + 2][lines]) for i in (0, 1)
                    )
                    scores = lax.dot_general(q, keys, NT, preferred_element_type=F32)
                    if t == tile_static:
                        scores = jnp.where(col <= row, scores, -1e30)
                    values = jnp.concatenate([values, jnp.ones((TILE, HD), BF)], 1)
                    state = fold(state, scores, values)
            at = 0
            size = TILE if first else rows_total
            while at < rows_total:
                scores = lax.dot_general(q, keys_ref[at:at + size], NT, preferred_element_type=F32)
                state = fold(state, scores, values_ref[at:at + size])
                at += size
            top, acc = state
            num, den = acc[:, :HD], acc[:, HD:]
            if not first:
                top = jnp.broadcast_to(top, (TILE, HD))
                old = jnp.broadcast_to(stat_in[:, h:h + 1], (TILE, HD))
                total = jnp.broadcast_to(stat_in[:, HEADS + h:HEADS + h + 1], (TILE, HD))
                new = jnp.maximum(old, top)
                keep, add = jnp.exp2((old - new) * SCALE), jnp.exp2((top - new) * SCALE)
                num = acc_in[:, cols] * keep + num * add
                den = total * keep + den * add
                top = new[:, :1]
            if last:
                row = tile * TILE + lax.broadcasted_iota(jnp.int32, (TILE, HD), 0)
                out_ref[:, cols] = jnp.where(row < length, num / den, 0.0).astype(BF)
            else:
                acc_out[:, cols] = num
                stat_out[:, h:h + 1] = top
                stat_out[:, HEADS + h:HEADS + h + 1] = den[:, :1]

    if first:
        for t in range(2):
            pl.when(live & (tile == t))(functools.partial(body, t))
    else:
        pl.when(live)(functools.partial(body, 0))

    if last:
        @pl.when(jnp.logical_not(live))
        def _():
            out_ref[...] = jnp.zeros_like(out_ref)


def attend(place, q_own, q_got, suffixes, kvs, state, samples, last, name):
    first = state is None
    rows, width = q_got.shape[0], q_got.shape[1] // 2
    counts = [kv.shape[0] for kv in kvs]
    keys_total = sum(kv.shape[0] * kv.shape[1] for kv in kvs)
    tiled = lambda w, base: pl.BlockSpec((None, TILE, w), lambda s, t, p: (base + s, t, 0))
    whole = lambda a: pl.BlockSpec(a.shape, lambda s, t, p: (0,) * a.ndim)
    in_specs = [
        pl.BlockSpec((TILE, width), lambda s, t, p: (t, p[CORE_AT])),
        pl.BlockSpec((TILE, width), lambda s, t, p: (t, p[CORE_AT])),
    ]
    args = [q_own, q_got]
    for array in ([*suffixes] if first else []) + kvs:
        in_specs.append(whole(array))
        args.append(array)
    if not first:
        in_specs += [tiled(width, samples[0]), tiled(HD, samples[0])]
        args += list(state)
    count = len(samples)
    if last:
        out_specs = tiled(width, 0)
        out_shape = jax.ShapeDtypeStruct((count, rows, width), BF)
    else:
        out_specs = [tiled(width, 0), tiled(HD, 0)]
        out_shape = [
            jax.ShapeDtypeStruct((count, rows, width), F32),
            jax.ShapeDtypeStruct((count, rows, HD), F32),
        ]
    keys_seen = keys_total + (rows // 2 if first else 0)
    return pl.pallas_call(
        functools.partial(attend_kernel, counts, samples, first, last),
        grid_spec=pltpu.PrefetchScalarGridSpec(
            num_scalar_prefetch=1,
            grid=(count, rows // TILE),
            in_specs=in_specs,
            out_specs=out_specs,
            scratch_shapes=[
                pltpu.VMEM((keys_total, HD), BF),
                pltpu.VMEM((keys_total, 2 * HD), BF),
            ],
        ),
        out_shape=out_shape,
        name=name,
        cost_estimate=pl.CostEstimate(
            flops=count * rows * HEADS * keys_seen * HD * 32,
            bytes_accessed=4 * count * 2**20,
            transcendentals=count * rows * HEADS * keys_seen,
        ),
        compiler_params=pltpu.CompilerParams(vmem_limit_bytes=48 * 2**20),
    )(place, *args)


OTHER, OWN = False, True
FEATURES = 320


def project_kernel(tiles, count, spans, outs, place_ref, *refs):
    weight_refs = refs[:2 * tiles]
    rows_refs = refs[2 * tiles:2 * tiles + 4 * count]
    add_refs = refs[2 * tiles + 4 * count:-1 - outs]
    out_refs, held_ref = refs[-1 - outs:-1], refs[-1]
    tile = pl.program_id(0)
    own = jnp.concatenate([r[...] for b in range(count) for r in rows_refs[4 * b:4 * b + 2]], axis=0)
    other = jnp.concatenate(
        [r[...] for b in range(count) for r in rows_refs[4 * b + 2:4 * b + 4]], axis=0
    )

    def bring(at):
        held_ref[0] = weight_refs[2 * at][...]
        held_ref[1] = weight_refs[2 * at + 1][...]

    for at in range(tiles):
        pl.when(tile == at)(functools.partial(bring, at))
    acc = lax.dot_general(held_ref[0], own, NT, preferred_element_type=F32)
    acc += lax.dot_general(held_ref[1], other, NT, preferred_element_type=F32)
    for ref, (start, length) in zip(add_refs, spans):
        here = (tile >= start) & (tile < start + length)
        acc += ref[...].astype(F32) if length == tiles else jnp.where(here, ref[...].astype(F32), 0.0)
    lanes = acc.shape[1] // outs
    for k, out_ref in enumerate(out_refs):
        out_ref[...] = acc[:, k * lanes:(k + 1) * lanes].astype(out_ref.dtype)


def project(place, weights, rows, blocks, adds, name, *kinds):
    tiles = len(weights)
    size = FEATURES
    kinds = kinds or (BF,)
    part, depth = rows[0].shape[1:]
    lanes = 2 * part * len(blocks)

    def rows_spec(step, own):
        def index(i, p):
            z = p[Z_HI] if own else 1 - p[Z_HI]
            return (2 * lax.rem(p[X] + step, 4) + z, 0, 0)

        return pl.BlockSpec((None, part, depth), index)

    def add_spec(lane, start, count):
        return pl.BlockSpec(
            (size, lanes), lambda i, p: (jnp.clip(i - start, 0, count - 1), lane)
        )

    in_specs, args = [], []
    for weight, at in weights:
        in_specs.append(pl.BlockSpec((size, depth), lambda i, p, at=at: (at, p[CORE_AT])))
        in_specs.append(pl.BlockSpec((size, depth), lambda i, p, at=at: (at, 1 - p[CORE_AT])))
        args += [weight, weight]
    for block in blocks:
        in_specs += [rows_spec(*block)] * 4
        args += rows
    for array, lane, start, count in adds:
        in_specs.append(add_spec(lane, start, count))
        args.append(array)
    wide = lanes // len(kinds)
    results = pl.pallas_call(
        functools.partial(project_kernel, tiles, len(blocks), [a[2:] for a in adds], len(kinds)),
        grid_spec=pltpu.PrefetchScalarGridSpec(
            num_scalar_prefetch=1,
            grid=(tiles,),
            in_specs=in_specs,
            out_specs=[pl.BlockSpec((size, wide), lambda i, p: (i, 0))] * len(kinds),
            scratch_shapes=[pltpu.VMEM((2, size, depth), BF)],
        ),
        out_shape=[jax.ShapeDtypeStruct((tiles * size, wide), kind) for kind in kinds],
        name=name,
        cost_estimate=pl.CostEstimate(
            flops=4 * tiles * size * lanes * depth,
            bytes_accessed=4 * tiles * size * depth + 2 * tiles * size * lanes,
            transcendentals=0,
        ),
        compiler_params=pltpu.CompilerParams(vmem_limit_bytes=32 * 2**20),
    )(place, *args)
    return results if len(kinds) > 1 else results[0]


def gather_kernel(count, base_ref, *refs):
    out_ref = refs[-1]
    halves, whole = refs[:-1 - count], refs[-1 - count:-1]
    lines = base_ref.shape[0] // 2
    for half in range(2):
        at = slice(half * lines, (half + 1) * lines)
        acc = base_ref[at]
        for ref in halves[half::2]:
            acc += ref[...].astype(F32)
        for ref in whole:
            acc += ref[at].astype(F32)
        out_ref[at] = acc.astype(BF)


def gather(base, lane, halves, whole, name):
    lines = base.shape[0]
    halves = [array for pair in halves for array in pair]
    spec = lambda size, at: pl.BlockSpec((size, 128), lambda i: (0, at))
    return pl.pallas_call(
        functools.partial(gather_kernel, len(whole)),
        grid=(1,),
        in_specs=[spec(lines, lane)] + [spec(lines // 2, lane)] * len(halves)
        + [spec(lines, 0)] * len(whole),
        out_specs=spec(lines, 0),
        out_shape=jax.ShapeDtypeStruct((lines, 128), BF),
        name=name,
        cost_estimate=pl.CostEstimate(
            flops=6 * lines * 128, bytes_accessed=20 * lines * 128, transcendentals=0
        ),
        compiler_params=pltpu.CompilerParams(vmem_limit_bytes=32 * 2**20),
    )(base, *halves, *whole)


def sum_over_head(place, weights, rows, tag, beside=()):
    run = lambda w, blocks, adds, name, *kinds: project(
        place, w, rows, blocks, adds, name + tag, *kinds
    )
    both = lambda step: [(step, OTHER), (step, OWN)]
    n = len(weights) // 2
    top, low = weights[:n], weights[n:]
    via_up = over_head(run(top, both(2), [], "far_top"), XUP)
    via_down = over_head(run(low, both(2), [], "far_low"), XDOWN)
    via_up, via_down, beside = lax.optimization_barrier((via_up, via_down, beside))
    below_low = over_head(run(low, both(1), [], "up_low"), XUP)
    above_top = over_head(run(top, both(3), [], "down_top"), XDOWN)
    below_top = over_head(run(top, both(1), [(via_up, 0, 0, n)], "up_top"), XUP)
    above_low = over_head(run(low, both(3), [(via_down, 0, 0, n)], "down_low"), XDOWN)
    own = run(weights, both(0), [], "own", F32)
    arrived = [(below_top, below_low), (above_top, above_low)]
    from_z = over_head(gather(own, 0, arrived, [], "give" + tag), ZHI)
    return from_z, lambda from_z: gather(own, 1, arrived, [from_z], "sum" + tag), beside


def give_z_first(place, weights, rows, tag):
    return project(place, weights, rows, [(step, OTHER) for step in range(4)], [], "give" + tag)


def sum_z_first(place, weights, rows, got, tag):
    steps = [(step, OWN) for step in range(4)]
    adds = [(got, 0, 0, len(weights))]
    return project(place, weights, rows, steps, adds, "steps" + tag, F32, BF, BF, BF)


EARLY_FROM = ((0, 0), (1, 0), (0, 3), (1, 3), (0, 1), (1, 1))
LATE_FROM = ((0, 2), (1, 2))


def finish_kernel(place_ref, from_ref, own_ref, got_ref, *refs):
    out_ref = refs[-1]
    lane = lax.broadcasted_iota(jnp.int32, (64, 128), 1)
    row = lax.broadcasted_iota(jnp.int32, (64, 128), 0)
    turn = lambda array, at: lax.dot_general(
        jnp.where(lane == row + at, 1.0, 0.0).astype(BF), array, NT, preferred_element_type=F32
    )
    own, got = turn(own_ref[...], 0), turn(got_ref[...], 64)
    first = place_ref[CORE_AT] == 0
    even, odd = jnp.where(first, own, got), jnp.where(first, got, own)
    out_ref[...] = jnp.concatenate([even, odd], axis=1).astype(BF)


def finish(place, own, got, chips, out, name):
    wide = 2 * FEATURES
    offsets = jnp.array([d for chip in chips for d in chip], jnp.int32)

    def to(i, p, f):
        z = lax.rem(f[2 * i] + p[Z_LO], 2)
        return (0, z * 4 + lax.rem(f[2 * i + 1] + p[Y], 4))

    part = pl.BlockSpec((FEATURES, 128), lambda i, p, f: (i, 0))
    return pl.pallas_call(
        finish_kernel,
        grid_spec=pltpu.PrefetchScalarGridSpec(
            num_scalar_prefetch=2,
            grid=(len(chips),),
            in_specs=[part, part] + [pl.BlockSpec(memory_space=pl.ANY)] * len(out),
            out_specs=pl.BlockSpec((64, wide), to),
        ),
        out_shape=jax.ShapeDtypeStruct((64, 8 * wide), BF),
        input_output_aliases={4: 0} if out else {},
        name=name,
        cost_estimate=pl.CostEstimate(
            flops=len(chips) * 2 * 64 * 128 * wide,
            bytes_accessed=len(chips) * wide * 400,
            transcendentals=0,
        ),
        compiler_params=pltpu.CompilerParams(vmem_limit_bytes=32 * 2**20),
    )(place, offsets, own, got, *out)


def per_device(
    queries, suffix_keys, suffix_values, prefix_keys, prefix_values, lengths, out_weight
):
    hold = lax.optimization_barrier
    sample = lax.axis_index("sample")
    head = lax.axis_index("head")
    core = sample % 2
    width = queries.shape[2] // 2
    place = jnp.stack([
        head // 2, head % 2, core, (sample // 2) % 4, sample // 8,
        lengths[sample], lengths[sample + 1 - 2 * core],
    ]).astype(jnp.int32)

    kv = jnp.concatenate([prefix_keys, prefix_values], axis=1)
    kv_z = over_sample(kv, ZLO)
    q_own = queries[0]
    q_got = over_sample(q_own, CORE)
    suffix = [suffix_keys[0], suffix_values[0]]
    suffixes = suffix + [over_sample(a, CORE) for a in suffix]
    kv_core = over_sample(kv, CORE)
    w, kv = hold((out_weight.T, kv))
    w_z = over_sample(w, ZLO)
    near = jnp.stack([kv, kv_z])
    ys = [over_sample(near, to) for to in (YUP, YDOWN, YFAR)]

    run = lambda kvs, state, samples, last, name: attend(
        place, q_own, q_got, suffixes, kvs, state, samples, last, name
    )
    state = run([kv[None], kv_core[None]], None, (0, 1), False, "attend_near")
    ys, state, w_z = hold((ys, state, w_z))
    w_pair = jnp.concatenate([w, w_z], axis=0)
    w_up, w_down = over_sample(w_pair, YUP), over_sample(w_pair, YDOWN)
    rest = [jnp.concatenate([kv_z[None]] + ys, axis=0)]
    rest_core = [over_sample(rest[0], CORE)]
    state = run(rest, state, (0, 1), False, "attend_far")
    own = run(rest_core, state, (0,), True, "attend_own")
    own_core = over_sample(own, CORE)
    state, own = hold((state, own))
    partner = run(rest_core, state, (1,), True, "attend_partner")
    partner_core = over_sample(partner, CORE)
    partner, w_up, w_down = hold((partner, w_up, w_down))
    w_far = over_sample(w_up[:FEATURES], YUP)
    wz_far = over_sample(w_down[FEATURES:], YDOWN)

    rows = [a.reshape(8, 64, width) for a in (own, partner, partner_core, own_core)]
    w_early = [(w_pair, 0), (w_pair, 1), (w_up, 0), (w_up, 1), (w_down, 0), (w_down, 1)]
    w_late = [(w_far, 0), (wz_far, 0)]
    give_late = give_z_first(place, w_late, rows, "_late")
    from_z, finish_early, give_late = sum_over_head(place, w_early, rows, "_early", give_late)
    got = over_head(give_late, ZHI)
    own, up, far, down = sum_z_first(place, w_late, rows, got, "_late")
    arrived = [over_head(far, XFAR), over_head(up, XUP), over_head(down, XDOWN)]
    from_z, arrived = hold((from_z, arrived))
    early = finish_early(from_z)
    late = gather(own, 0, [], arrived, "sum_late")

    out = finish(place, early, over_sample(early, CORE), EARLY_FROM, [], "finish_early")
    out = finish(place, late, over_sample(late, CORE), LATE_FROM, [out], "finish_late")
    return out[None]


def solution(mesh):
    placed = (
        P("sample", None, "head"),
        P("sample", None, "head"),
        P("sample", None, "head"),
        P("sample", "head"),
        P("sample", "head"),
        P(),
        P("head", "sample"),
    )
    return jax.shard_map(
        per_device, mesh=mesh, in_specs=placed, out_specs=P("sample", "head", None), check_vma=False
    )
```

```python
import functools
import math

import jax
import jax.numpy as jnp
from jax import lax
from jax.experimental import pallas as pl
from jax.experimental.pallas import tpu as pltpu
from jax.sharding import PartitionSpec as P

HD = 128
HEADS = 4
TILE = 256
SCALE = HD ** (-0.5) * math.log2(math.e)
BF = jnp.bfloat16
F32 = jnp.float32
NT = (((1,), (1,)), ((), ()))


def sample_pairs(to):
    place = lambda z, y, c: (z * 4 + y) * 2 + c
    return [
        (place(z, y, c), place(*to(z, y, c)))
        for z in range(2) for y in range(4) for c in range(2)
    ]


def head_pairs(to):
    pairs = []
    for x in range(4):
        for z in range(2):
            tx, tz = to(x, z)
            pairs.append((x * 2 + z, tx * 2 + tz))
    return pairs


CORE = sample_pairs(lambda z, y, c: (z, y, 1 - c))
ZLO = sample_pairs(lambda z, y, c: (1 - z, y, c))
YUP = sample_pairs(lambda z, y, c: (z, (y + 1) % 4, c))
YDOWN = sample_pairs(lambda z, y, c: (z, (y + 3) % 4, c))
YFAR = sample_pairs(lambda z, y, c: (z, (y + 2) % 4, c))
XUP = head_pairs(lambda x, z: ((x + 1) % 4, z))
XDOWN = head_pairs(lambda x, z: ((x + 3) % 4, z))
XFAR = head_pairs(lambda x, z: ((x + 2) % 4, z))
ZHI = head_pairs(lambda x, z: (x, 1 - z))


def over_sample(value, pairs):
    return lax.ppermute(value, "sample", pairs)


def over_head(value, pairs):
    return lax.ppermute(value, "head", pairs)


X, Z_HI, CORE_AT, Y, Z_LO, LENGTH = range(6)


def attend_kernel(counts, samples, first, last, place_ref, q_own_ref, q_got_ref, *refs):
    refs = list(refs)
    suffix_refs = [refs.pop(0) for _ in range(4)] if first else None
    kv_refs = [refs.pop(0) for _ in counts]
    acc_in, stat_in = (None, None) if first else (refs.pop(0), refs.pop(0))
    if last:
        out_ref = refs.pop(0)
    else:
        acc_out, stat_out = refs.pop(0), refs.pop(0)
    keys_ref, values_ref = refs.pop(0), refs.pop(0)
    step, tile = pl.program_id(0), pl.program_id(1)
    sample = samples[0] + step
    rows_total = keys_ref.shape[0]

    @pl.when((step == 0) & (tile == 0))
    def _():
        at = 0
        for kv_ref, count in zip(kv_refs, counts):
            for b in range(count):
                block = kv_ref[b]
                rows = block.shape[0]
                keys_ref[at:at + rows] = block[:, :HD]
                values_ref[at:at + rows, :HD] = block[:, HD:]
                at += rows
        values_ref[:, HD:] = jnp.ones((rows_total, HD), BF)

    length = place_ref[LENGTH + sample]
    live = tile * TILE < length

    def pick(own, got):
        if len(samples) == 1:
            return got if samples[0] else own
        return jnp.where(sample == 0, own, got)

    def fold(state, scores, values):
        top = jnp.max(scores, axis=1, keepdims=True)
        if state is None:
            weights = jnp.exp2((scores - top) * SCALE)
            return top, jnp.dot(weights.astype(BF), values, preferred_element_type=F32)
        old, acc = state
        top = jnp.maximum(old, top)
        weights = jnp.exp2((scores - top) * SCALE)
        part = jnp.dot(weights.astype(BF), values, preferred_element_type=F32)
        return top, acc * jnp.exp2((old - top) * SCALE) + part

    def body(tile_static):
        for h in range(HEADS):
            cols = slice(h * HD, (h + 1) * HD)
            q = pick(q_own_ref[:, cols], q_got_ref[:, cols])
            state = None
            if first:
                row = lax.broadcasted_iota(jnp.int32, (TILE, TILE), 0)
                col = lax.broadcasted_iota(jnp.int32, (TILE, TILE), 1)
                for t in range(tile_static, -1, -1):
                    lines = slice(t * TILE, (t + 1) * TILE)
                    keys, values = (
                        pick(suffix_refs[i][lines], suffix_refs[i + 2][lines]) for i in (0, 1)
                    )
                    scores = lax.dot_general(q, keys, NT, preferred_element_type=F32)
                    if t == tile_static:
                        scores = jnp.where(col <= row, scores, -1e30)
                    values = jnp.concatenate([values, jnp.ones((TILE, HD), BF)], 1)
                    state = fold(state, scores, values)
            at = 0
            size = TILE if first else rows_total
            while at < rows_total:
                scores = lax.dot_general(q, keys_ref[at:at + size], NT, preferred_element_type=F32)
                state = fold(state, scores, values_ref[at:at + size])
                at += size
            top, acc = state
            num, den = acc[:, :HD], acc[:, HD:]
            if not first:
                top = jnp.broadcast_to(top, (TILE, HD))
                old = jnp.broadcast_to(stat_in[:, h:h + 1], (TILE, HD))
                total = jnp.broadcast_to(stat_in[:, HEADS + h:HEADS + h + 1], (TILE, HD))
                new = jnp.maximum(old, top)
                keep, add = jnp.exp2((old - new) * SCALE), jnp.exp2((top - new) * SCALE)
                num = acc_in[:, cols] * keep + num * add
                den = total * keep + den * add
                top = new[:, :1]
            if last:
                row = tile * TILE + lax.broadcasted_iota(jnp.int32, (TILE, HD), 0)
                out_ref[:, cols] = jnp.where(row < length, num / den, 0.0).astype(BF)
            else:
                acc_out[:, cols] = num
                stat_out[:, h:h + 1] = top
                stat_out[:, HEADS + h:HEADS + h + 1] = den[:, :1]

    if first:
        for t in range(2):
            pl.when(live & (tile == t))(functools.partial(body, t))
    else:
        pl.when(live)(functools.partial(body, 0))

    if last:
        @pl.when(jnp.logical_not(live))
        def _():
            out_ref[...] = jnp.zeros_like(out_ref)


def attend(place, q_own, q_got, suffixes, kvs, state, samples, last, name):
    first = state is None
    rows, width = q_got.shape[0], q_got.shape[1] // 2
    counts = [kv.shape[0] for kv in kvs]
    keys_total = sum(kv.shape[0] * kv.shape[1] for kv in kvs)
    tiled = lambda w, base: pl.BlockSpec((None, TILE, w), lambda s, t, p: (base + s, t, 0))
    whole = lambda a: pl.BlockSpec(a.shape, lambda s, t, p: (0,) * a.ndim)
    in_specs = [
        pl.BlockSpec((TILE, width), lambda s, t, p: (t, p[CORE_AT])),
        pl.BlockSpec((TILE, width), lambda s, t, p: (t, p[CORE_AT])),
    ]
    args = [q_own, q_got]
    for array in ([*suffixes] if first else []) + kvs:
        in_specs.append(whole(array))
        args.append(array)
    if not first:
        in_specs += [tiled(width, samples[0]), tiled(HD, samples[0])]
        args += list(state)
    count = len(samples)
    if last:
        out_specs = tiled(width, 0)
        out_shape = jax.ShapeDtypeStruct((count, rows, width), BF)
    else:
        out_specs = [tiled(width, 0), tiled(HD, 0)]
        out_shape = [
            jax.ShapeDtypeStruct((count, rows, width), F32),
            jax.ShapeDtypeStruct((count, rows, HD), F32),
        ]
    keys_seen = keys_total + (rows // 2 if first else 0)
    return pl.pallas_call(
        functools.partial(attend_kernel, counts, samples, first, last),
        grid_spec=pltpu.PrefetchScalarGridSpec(
            num_scalar_prefetch=1,
            grid=(count, rows // TILE),
            in_specs=in_specs,
            out_specs=out_specs,
            scratch_shapes=[
                pltpu.VMEM((keys_total, HD), BF),
                pltpu.VMEM((keys_total, 2 * HD), BF),
            ],
        ),
        out_shape=out_shape,
        name=name,
        cost_estimate=pl.CostEstimate(
            flops=count * rows * HEADS * keys_seen * HD * 32,
            bytes_accessed=4 * count * 2**20,
            transcendentals=count * rows * HEADS * keys_seen,
        ),
        compiler_params=pltpu.CompilerParams(vmem_limit_bytes=48 * 2**20),
    )(place, *args)


OTHER, OWN = False, True
FEATURES = 320


def project_kernel(tiles, count, spans, outs, place_ref, *refs):
    weight_refs = refs[:2 * tiles]
    rows_refs = refs[2 * tiles:2 * tiles + 4 * count]
    add_refs = refs[2 * tiles + 4 * count:-1 - outs]
    out_refs, held_ref = refs[-1 - outs:-1], refs[-1]
    tile = pl.program_id(0)
    own = jnp.concatenate([r[...] for b in range(count) for r in rows_refs[4 * b:4 * b + 2]], axis=0)
    other = jnp.concatenate(
        [r[...] for b in range(count) for r in rows_refs[4 * b + 2:4 * b + 4]], axis=0
    )

    def bring(at):
        held_ref[0] = weight_refs[2 * at][...]
        held_ref[1] = weight_refs[2 * at + 1][...]

    for at in range(tiles):
        pl.when(tile == at)(functools.partial(bring, at))
    acc = lax.dot_general(held_ref[0], own, NT, preferred_element_type=F32)
    acc += lax.dot_general(held_ref[1], other, NT, preferred_element_type=F32)
    for ref, (start, length) in zip(add_refs, spans):
        here = (tile >= start) & (tile < start + length)
        acc += ref[...].astype(F32) if length == tiles else jnp.where(here, ref[...].astype(F32), 0.0)
    lanes = acc.shape[1] // outs
    for k, out_ref in enumerate(out_refs):
        out_ref[...] = acc[:, k * lanes:(k + 1) * lanes].astype(out_ref.dtype)


def project(place, weights, rows, blocks, adds, name, *kinds):
    tiles = len(weights)
    size = FEATURES
    kinds = kinds or (BF,)
    part, depth = rows[0].shape[1:]
    lanes = 2 * part * len(blocks)

    def rows_spec(step, own):
        def index(i, p):
            z = p[Z_HI] if own else 1 - p[Z_HI]
            return (2 * lax.rem(p[X] + step, 4) + z, 0, 0)

        return pl.BlockSpec((None, part, depth), index)

    def add_spec(lane, start, count):
        return pl.BlockSpec(
            (size, lanes), lambda i, p: (jnp.clip(i - start, 0, count - 1), lane)
        )

    in_specs, args = [], []
    for weight, at in weights:
        in_specs.append(pl.BlockSpec((size, depth), lambda i, p, at=at: (at, p[CORE_AT])))
        in_specs.append(pl.BlockSpec((size, depth), lambda i, p, at=at: (at, 1 - p[CORE_AT])))
        args += [weight, weight]
    for block in blocks:
        in_specs += [rows_spec(*block)] * 4
        args += rows
    for array, lane, start, count in adds:
        in_specs.append(add_spec(lane, start, count))
        args.append(array)
    wide = lanes // len(kinds)
    results = pl.pallas_call(
        functools.partial(project_kernel, tiles, len(blocks), [a[2:] for a in adds], len(kinds)),
        grid_spec=pltpu.PrefetchScalarGridSpec(
            num_scalar_prefetch=1,
            grid=(tiles,),
            in_specs=in_specs,
            out_specs=[pl.BlockSpec((size, wide), lambda i, p: (i, 0))] * len(kinds),
            scratch_shapes=[pltpu.VMEM((2, size, depth), BF)],
        ),
        out_shape=[jax.ShapeDtypeStruct((tiles * size, wide), kind) for kind in kinds],
        name=name,
        cost_estimate=pl.CostEstimate(
            flops=4 * tiles * size * lanes * depth,
            bytes_accessed=4 * tiles * size * depth + 2 * tiles * size * lanes,
            transcendentals=0,
        ),
        compiler_params=pltpu.CompilerParams(vmem_limit_bytes=32 * 2**20),
    )(place, *args)
    return results if len(kinds) > 1 else results[0]


def gather_kernel(count, base_ref, *refs):
    out_ref = refs[-1]
    halves, whole = refs[:-1 - count], refs[-1 - count:-1]
    lines = base_ref.shape[0] // 2
    for half in range(2):
        at = slice(half * lines, (half + 1) * lines)
        acc = base_ref[at]
        for ref in halves[half::2]:
            acc += ref[...].astype(F32)
        for ref in whole:
            acc += ref[at].astype(F32)
        out_ref[at] = acc.astype(BF)


def gather(base, lane, halves, whole, name):
    lines = base.shape[0]
    halves = [array for pair in halves for array in pair]
    spec = lambda size, at: pl.BlockSpec((size, 128), lambda i: (0, at))
    return pl.pallas_call(
        functools.partial(gather_kernel, len(whole)),
        grid=(1,),
        in_specs=[spec(lines, lane)] + [spec(lines // 2, lane)] * len(halves)
        + [spec(lines, 0)] * len(whole),
        out_specs=spec(lines, 0),
        out_shape=jax.ShapeDtypeStruct((lines, 128), BF),
        name=name,
        cost_estimate=pl.CostEstimate(
            flops=6 * lines * 128, bytes_accessed=20 * lines * 128, transcendentals=0
        ),
        compiler_params=pltpu.CompilerParams(vmem_limit_bytes=32 * 2**20),
    )(base, *halves, *whole)


def sum_over_head(place, weights, rows, tag, beside=()):
    run = lambda w, blocks, adds, name, *kinds: project(
        place, w, rows, blocks, adds, name + tag, *kinds
    )
    both = lambda step: [(step, OTHER), (step, OWN)]
    n = len(weights) // 2
    top, low = weights[:n], weights[n:]
    via_up = over_head(run(top, both(2), [], "far_top"), XUP)
    via_down = over_head(run(low, both(2), [], "far_low"), XDOWN)
    via_up, via_down, beside = lax.optimization_barrier((via_up, via_down, beside))
    below_low = over_head(run(low, both(1), [], "up_low"), XUP)
    above_top = over_head(run(top, both(3), [], "down_top"), XDOWN)
    below_top = over_head(run(top, both(1), [(via_up, 0, 0, n)], "up_top"), XUP)
    above_low = over_head(run(low, both(3), [(via_down, 0, 0, n)], "down_low"), XDOWN)
    own = run(weights, both(0), [], "own", F32)
    arrived = [(below_top, below_low), (above_top, above_low)]
    from_z = over_head(gather(own, 0, arrived, [], "give" + tag), ZHI)
    return from_z, lambda from_z: gather(own, 1, arrived, [from_z], "sum" + tag), beside


def give_z_first(place, weights, rows, tag):
    return project(place, weights, rows, [(step, OTHER) for step in range(4)], [], "give" + tag)


def sum_z_first(place, weights, rows, got, tag):
    steps = [(step, OWN) for step in range(4)]
    adds = [(got, 0, 0, len(weights))]
    return project(place, weights, rows, steps, adds, "steps" + tag, F32, BF, BF, BF)


EARLY_FROM = ((0, 0), (1, 0), (0, 3), (1, 3), (0, 1), (1, 1))
LATE_FROM = ((0, 2), (1, 2))


def finish_kernel(place_ref, own_early_ref, own_late_ref, got_early_ref, got_late_ref, out_ref):
    first = place_ref[CORE_AT] == 0
    wide = 2 * FEATURES
    for own_ref, got_ref, chips in (
        (own_early_ref, got_early_ref, EARLY_FROM), (own_late_ref, got_late_ref, LATE_FROM)
    ):
        for at, (dz, dy) in enumerate(chips):
            lines = slice(at * FEATURES, (at + 1) * FEATURES)
            own = jnp.transpose(own_ref[lines].astype(F32))[:64]
            got = jnp.transpose(got_ref[lines].astype(F32))[64:]
            even, odd = jnp.where(first, own, got), jnp.where(first, got, own)
            z = lax.rem(place_ref[Z_LO] + dz, 2)
            to = (z * 4 + lax.rem(place_ref[Y] + dy, 4)) * wide
            columns = pl.ds(pl.multiple_of(to, 128), wide)
            out_ref[:, columns] = jnp.concatenate([even, odd], axis=1).astype(BF)


def finish(place, own, got):
    whole = [pl.BlockSpec(a.shape, lambda i, p: (0, 0)) for a in own + got]
    columns = 2 * FEATURES * (len(EARLY_FROM) + len(LATE_FROM))
    return pl.pallas_call(
        finish_kernel,
        grid_spec=pltpu.PrefetchScalarGridSpec(
            num_scalar_prefetch=1,
            grid=(1,),
            in_specs=whole,
            out_specs=pl.BlockSpec((64, columns), lambda i, p: (0, 0)),
        ),
        out_shape=jax.ShapeDtypeStruct((64, columns), BF),
        name="finish",
        compiler_params=pltpu.CompilerParams(vmem_limit_bytes=60 * 2**20),
    )(place, *own, *got)


def per_device(
    queries, suffix_keys, suffix_values, prefix_keys, prefix_values, lengths, out_weight
):
    hold = lax.optimization_barrier
    sample = lax.axis_index("sample")
    head = lax.axis_index("head")
    core = sample % 2
    width = queries.shape[2] // 2
    place = jnp.stack([
        head // 2, head % 2, core, (sample // 2) % 4, sample // 8,
        lengths[sample], lengths[sample + 1 - 2 * core],
    ]).astype(jnp.int32)

    kv = jnp.concatenate([prefix_keys, prefix_values], axis=1)
    kv_z = over_sample(kv, ZLO)
    q_own = queries[0]
    q_got = over_sample(q_own, CORE)
    suffix = [suffix_keys[0], suffix_values[0]]
    suffixes = suffix + [over_sample(a, CORE) for a in suffix]
    kv_core = over_sample(kv, CORE)
    w, kv = hold((out_weight.T, kv))
    w_z = over_sample(w, ZLO)
    near = jnp.stack([kv, kv_z])
    ys = [over_sample(near, to) for to in (YUP, YDOWN, YFAR)]

    run = lambda kvs, state, samples, last, name: attend(
        place, q_own, q_got, suffixes, kvs, state, samples, last, name
    )
    state = run([kv[None], kv_core[None]], None, (0, 1), False, "attend_near")
    ys[0], state, w_z = hold((ys[0], state, w_z))
    w_pair = jnp.concatenate([w, w_z], axis=0)
    w_up, w_down = over_sample(w_pair, YUP), over_sample(w_pair, YDOWN)
    rest = [jnp.concatenate([kv_z[None]] + ys, axis=0)]
    rest_core = [over_sample(rest[0], CORE)]
    state = run(rest, state, (0, 1), False, "attend_far")
    own = run(rest_core, state, (0,), True, "attend_own")
    own_core = over_sample(own, CORE)
    state, own = hold((state, own))
    partner = run(rest_core, state, (1,), True, "attend_partner")
    partner_core = over_sample(partner, CORE)
    partner, w_up, w_down = hold((partner, w_up, w_down))
    w_far = over_sample(w_up[:FEATURES], YUP)
    wz_far = over_sample(w_down[FEATURES:], YDOWN)

    rows = [a.reshape(8, 64, width) for a in (own, partner, partner_core, own_core)]
    w_early = [(w_pair, 0), (w_pair, 1), (w_up, 0), (w_up, 1), (w_down, 0), (w_down, 1)]
    w_late = [(w_far, 0), (wz_far, 0)]
    give_late = give_z_first(place, w_late, rows, "_late")
    from_z, finish_early, give_late = sum_over_head(place, w_early, rows, "_early", give_late)
    got = over_head(give_late, ZHI)
    own, up, far, down = sum_z_first(place, w_late, rows, got, "_late")
    arrived = [over_head(far, XFAR), over_head(up, XUP), over_head(down, XDOWN)]
    from_z, arrived = hold((from_z, arrived))
    early = finish_early(from_z)
    late = gather(own, 0, [], arrived, "sum_late")

    got = [over_sample(early, CORE), over_sample(late, CORE)]
    return finish(place, [early, late], got)[None]


def solution(mesh):
    placed = (
        P("sample", None, "head"),
        P("sample", None, "head"),
        P("sample", None, "head"),
        P("sample", "head"),
        P("sample", "head"),
        P(),
        P("head", "sample"),
    )
    return jax.shard_map(
        per_device, mesh=mesh, in_specs=placed, out_specs=P("sample", "head", None), check_vma=False
    )
```
